512 devices in a mesh: walker: 32 (over x, z), tangent: 16 (over y, core).
Axes of the slice: x: 4, y: 8, z: 8, core: 2. Of those that a mesh axis runs over, the one named last changes fastest.
Arguments:
- hidden0: float32 [64, 120, 256], P('walker'), may hold values from -6 to 6
- tangent0: bfloat16 [64, 256, 120, 256], P('walker', 'tangent'), may hold values from -0.5 to 0.5
- laplace0: float32 [64, 120, 256], P('walker'), may hold values from -6 to 6
- spins: int32 [64, 120], P('walker'), may hold values from 0 to 1
- weights: bfloat16 [2, 256, 256], replicated, may hold values from -0.375 to 0.375
- spin_bias: float32 [2, 2, 256], replicated, may hold values from -3 to 3
- readout: float32 [256], replicated, may hold values from -0.03125 to 0.03125
- energy_cotangent: float32 [64], P('walker'), may hold values from -4 to 4
Outputs:
- energy: float32 [64], P('walker')
- grad_weights: float32 [2, 256, 256], P(None, 'tangent')
- grad_bias: float32 [2, 2, 256], replicated
- grad_readout: float32 [256], replicated
The draws below stay inside these ranges and needn't reach their ends.
All inputs are finite; a program needn't handle non-finite values.
Results may differ from the reference program's by a relative error of at most 0.0094.
Values sent between devices are 32-bit elements; how exact they have to be, the bound alone decides.
No kernel may reach another device: no remote copies, remote signals or barrier semaphores. Data moves between devices by JAX's collectives and lax.ppermute only.
A program may use at most 64 MiB of HBM per device.

```python
import jax
import jax.numpy as jnp
from jax import lax

NE = 120
D = 256
LAYERS = 2
WALKERS = 64
TANGENTS = 256


def draw_tangent0(key, part):
    key = jax.random.fold_in(key, 7)
    shape = (WALKERS, TANGENTS, NE, D)
    level = jnp.arange(TANGENTS, dtype=jnp.float32) / max(TANGENTS - 1, 1)
    spread = ((1.0 + 2.0 * level) / 24.0)[None, :, None, None]
    values = jnp.clip(jax.random.normal(key, shape, jnp.float32), -4.0, 4.0)
    return jnp.clip(values * spread, -0.5, 0.5).astype(jnp.bfloat16)


def place_ends(values, key, smallest, high):
    longest = values.shape.index(max(values.shape))
    spots = []
    for shift in (0, 1):
        where = [jax.random.randint(jax.random.fold_in(key, axis), (), 0, length) for axis, length in enumerate(values.shape)]
        where[longest] = (where[longest] + shift) % values.shape[longest]
        spots.append(tuple(where))
    return values.at[spots[0]].set(smallest).at[spots[1]].set(high)


def block_levels(stream_key, dims, cuts, low, high):
    loudness = 1.0
    for position, shards_of in cuts:
        draws = jax.random.uniform(jax.random.fold_in(jax.random.fold_in(stream_key, 6), position), (shards_of,), jnp.float32, low / len(cuts), high / len(cuts))
        loudness = loudness * jnp.repeat(jnp.exp(draws), dims[position] // shards_of).reshape((-1,) + (1,) * (len(dims) - 1 - position))
    return loudness


def normal_values(own_key, shape, scale, limit, pieces=(), held_as=jnp.bfloat16):
    drawn = scale * jax.random.normal(own_key, shape, jnp.float32)
    if pieces:
        drawn = drawn * block_levels(own_key, shape, pieces, -0.22, 0.18)
    return jnp.clip(drawn, -limit, limit).astype(held_as)


def setup_inputs(seed: int = 0) -> dict:
    streams_of = jax.random.split(jax.random.key(seed), 9)
    return {
        "hidden0": normal_values(streams_of[0], (WALKERS, NE, D), 1.0, 6.0, ((0, 32),), jnp.float32),
        "tangent0": draw_tangent0(jax.random.fold_in(streams_of[8], 71), 0),
        "laplace0": normal_values(streams_of[2], (WALKERS, NE, D), 1.0, 6.0, ((0, 32),), jnp.float32),
        "spins": place_ends(jax.random.randint(streams_of[3], (WALKERS, NE), 0, 2), jax.random.fold_in(streams_of[3], 1), 0, 1).astype(jnp.int32),
        "weights": normal_values(streams_of[4], (LAYERS, D, D), D ** -0.5, 0.375),
        "spin_bias": normal_values(streams_of[5], (LAYERS, 2, D), 0.5, 3.0, (), jnp.float32),
        "readout": normal_values(streams_of[6], (D,), (NE * D) ** -0.5, 0.03125, (), jnp.float32),
        "energy_cotangent": normal_values(streams_of[7], (WALKERS,), 1.0, 4.0, ((0, 32),), jnp.float32),
    }


def outer(left, right):
    width = right.shape[-1]
    return lax.dot_general(left.reshape(-1, left.shape[-1]), right.reshape(-1, width), (((0,), (0,)), ((), ())), preferred_element_type=jnp.float32)


def walker_block(hidden, tangents, laplace, spins, weights, spin_bias, readout, coeff):
    stored = []
    for layer in range(LAYERS):
        weight = weights[layer]
        table = spin_bias[layer]
        hid_b = hidden.astype(jnp.bfloat16)
        lap_b = laplace.astype(jnp.bfloat16)
        bias = jnp.where(spins[..., None] == 0, table[0], table[1])
        pre = jnp.dot(hid_b, weight, preferred_element_type=jnp.float32) + bias
        images = jnp.dot(tangents, weight, preferred_element_type=jnp.float32)
        lap_image = jnp.dot(lap_b, weight, preferred_element_type=jnp.float32)
        act = jnp.tanh(pre)
        slope = 1.0 - act * act
        curve = -2.0 * act * slope
        squares = jnp.sum(images * images, axis=1)
        stored.append((hid_b, tangents, lap_b, act, slope, curve, images, lap_image, squares))
        hidden = hidden + act
        laplace = laplace + slope * lap_image + curve * squares
        tangents = (tangents.astype(jnp.float32) + slope[:, None] * images).astype(jnp.bfloat16)
    tang_f = tangents.astype(jnp.float32)
    grads_t = jnp.sum(tang_f * readout, axis=(2, 3))
    lap_val = jnp.sum(laplace * readout, axis=(1, 2))
    energy = -0.5 * (lap_val + jnp.sum(grads_t * grads_t, axis=1))
    scaled = coeff[:, None] * grads_t
    grad_read = -0.5 * jnp.sum(coeff[:, None, None] * laplace, axis=(0, 1)) - jnp.sum(scaled[:, :, None, None] * tang_f, axis=(0, 1, 2))
    g_lap = -0.5 * coeff[:, None, None] * jnp.ones_like(laplace) * readout
    g_tan = -scaled[:, :, None, None] * readout
    g_hid = jnp.zeros_like(hidden)
    grad_w = [None] * LAYERS
    grad_b = [None] * LAYERS
    for layer in reversed(range(LAYERS)):
        hid_b, tang_in, lap_b, act, slope, curve, images, lap_image, squares = stored[layer]
        weight = weights[layer]
        g_lap_image = slope * g_lap
        g_images = slope[:, None] * g_tan + 2.0 * (curve * g_lap)[:, None] * images
        g_slope = g_lap * lap_image + jnp.sum(g_tan * images, axis=1)
        g_act = -2.0 * act * g_slope + (6.0 * act * act - 2.0) * g_lap * squares + g_hid
        g_pre = g_act * slope
        g_pre_b = g_pre.astype(jnp.bfloat16)
        g_images_b = g_images.astype(jnp.bfloat16)
        g_lap_image_b = g_lap_image.astype(jnp.bfloat16)
        grad_w[layer] = outer(hid_b, g_pre_b) + outer(tang_in, g_images_b) + outer(lap_b, g_lap_image_b)
        first_spin = jnp.sum(jnp.where(spins[..., None] == 0, g_pre, 0.0), axis=(0, 1))
        second_spin = jnp.sum(jnp.where(spins[..., None] == 1, g_pre, 0.0), axis=(0, 1))
        grad_b[layer] = jnp.stack([first_spin, second_spin])
        if layer > 0:
            g_hid = g_hid + jnp.dot(g_pre_b, weight.T, preferred_element_type=jnp.float32)
            g_tan = g_tan + jnp.dot(g_images_b, weight.T, preferred_element_type=jnp.float32)
            g_lap = g_lap + jnp.dot(g_lap_image_b, weight.T, preferred_element_type=jnp.float32)
    return energy, jnp.stack(grad_w), jnp.stack(grad_b), grad_read


def reference(hidden0, tangent0, laplace0, spins, weights, spin_bias, readout, energy_cotangent):
    coeff = energy_cotangent / WALKERS

    def advance(carry, item):
        hidden, tangents, laplace, spin_row, factor = item
        energy, grad_w, grad_b, grad_read = walker_block(hidden[None], tangents[None], laplace[None], spin_row[None], weights, spin_bias, readout, factor[None])
        return (carry[0] + grad_w, carry[1] + grad_b, carry[2] + grad_read), energy[0]

    start = (jnp.zeros((LAYERS, D, D), jnp.float32), jnp.zeros((LAYERS, 2, D), jnp.float32), jnp.zeros((D,), jnp.float32))
    totals, energies = lax.scan(advance, start, (hidden0, tangent0, laplace0, spins, coeff))
    return energies, totals[0], totals[1], totals[2]
```

```python
import functools

import jax
import jax.numpy as jnp
from jax import lax
from jax.experimental import pallas as pl
from jax.experimental.pallas import tpu as pltpu
from jax.sharding import Mesh, PartitionSpec as P

NX, NZ, NY, NC = 4, 8, 8, 2
GROUP = NY * NC
CHUNK = 4
F32 = jnp.float32
BF16 = jnp.bfloat16


def mm(a, b):
    return lax.dot_general(a, b, (((1,), (0,)), ((), ())), preferred_element_type=F32)


def outer(a, b):
    return lax.dot_general(a, b, (((0,), (0,)), ((), ())), preferred_element_type=F32)


def local_kernel(cot_ref, tan_ref, hid_ref, lap_ref, spin_ref, w_ref, bias_ref, read_ref, out_ref,
                 wt_ref, a0_ref, a1_ref, s0_ref, s1_ref, amp1_ref, b1_ref, b0_ref, gl1_ref, h1_ref,
                 sq0_ref, sq1_ref, x0_ref, x1_ref, gw_ref, acc_ref, *, walkers, ne, width, walkers_all):
    w = pl.program_id(0)
    k = pl.program_id(1)
    rows = walkers * ne
    read = read_ref[...]

    def coeff(i):
        return cot_ref[i] * (1.0 / walkers_all)

    @pl.when((w == 0) & (k == 0))
    def _():
        wt_ref[...] = w_ref[1].T
        spin = spin_ref[...]
        hid0 = hid_ref[...]

        def layer(hid, l):
            bias = jnp.where(spin == 0, bias_ref[l, 0:1, :], bias_ref[l, 1:2, :])
            return jnp.tanh(mm(hid.astype(BF16), w_ref[l]) + bias)

        a0 = layer(hid0, 0)
        h1 = hid0 + a0
        a1 = layer(h1, 1)
        a0_ref[...] = a0
        a1_ref[...] = a1
        h1_ref[...] = h1.astype(BF16)
        s0 = 1.0 - a0 * a0
        s1 = 1.0 - a1 * a1
        s0_ref[...] = s0
        s1_ref[...] = s1
        cr = jnp.concatenate([jnp.broadcast_to(coeff(i) * read, (ne, width)) for i in range(walkers)], axis=0)
        gl2 = -0.5 * cr
        amp1_ref[...] = -cr * s1
        b1_ref[...] = 2.0 * cr * a1 * s1
        gl1 = gl2 + mm((s1 * gl2).astype(BF16), wt_ref[...])
        gl1_ref[...] = gl1
        b0_ref[...] = -4.0 * a0 * s0 * gl1
        sq0_ref[...] = jnp.zeros_like(sq0_ref)
        sq1_ref[...] = jnp.zeros_like(sq1_ref)
        x0_ref[...] = jnp.zeros_like(x0_ref)
        x1_ref[...] = jnp.zeros_like(x1_ref)
        gw_ref[...] = jnp.zeros_like(gw_ref)
        acc_ref[...] = jnp.zeros_like(acc_ref)

    c = coeff(w)
    here = pl.ds(pl.multiple_of(w * ne, 8), ne)
    s0 = s0_ref[here]
    s1 = s1_ref[here]
    tan0 = tan_ref[...]

    def split(v):
        return v.reshape(CHUNK, ne, width)

    def flat(v):
        return v.reshape(CHUNK * ne, width)

    z0 = split(mm(tan0, w_ref[0]))
    sq0_ref[here] += jnp.sum(z0 * z0, axis=0)
    tan1 = flat(split(tan0.astype(F32)) + s0[None] * z0).astype(BF16)
    z1 = split(mm(tan1, w_ref[1]))
    sq1_ref[here] += jnp.sum(z1 * z1, axis=0)
    tan2 = split(tan1.astype(F32)) + s1[None] * z1
    tan2 = tan2.astype(BF16).astype(F32)
    cols = jnp.sum(tan2, axis=1)
    g = jnp.sum(cols * read, axis=1, keepdims=True)
    acc_ref[pl.ds(w, 1), 0:1, :] += jnp.broadcast_to(jnp.sum(g * g, axis=0, keepdims=True), (1, width))[None]
    acc_ref[pl.ds(w, 1), 1:2, :] += jnp.sum(g * cols, axis=0, keepdims=True)[None]
    gt = g[:, :, None]
    x1_ref[here] += jnp.sum(gt * z1, axis=0)
    gz1 = flat(gt * amp1_ref[here][None] + b1_ref[here][None] * z1).astype(BF16)
    gw_ref[1] += outer(tan1, gz1)
    gt1 = split(mm(gz1, wt_ref[...])) - (c * gt) * read[None]
    x0_ref[here] += jnp.sum(gt1 * z0, axis=0)
    gz0 = flat(s0[None] * gt1 + b0_ref[here][None] * z0).astype(BF16)
    gw_ref[0] += outer(tan0, gz0)

    @pl.when((w == pl.num_programs(0) - 1) & (k == pl.num_programs(1) - 1))
    def _():
        share = 1.0 / GROUP
        spin = spin_ref[...]
        cr = jnp.concatenate([jnp.broadcast_to(coeff(i) * read, (ne, width)) for i in range(walkers)], axis=0)
        gl2 = -0.5 * cr
        a0, a1, s0, s1, gl1 = a0_ref[...], a1_ref[...], s0_ref[...], s1_ref[...], gl1_ref[...]
        sq0, sq1 = sq0_ref[...], sq1_ref[...]
        lap0 = lap_ref[...]
        lb0 = lap0.astype(BF16)
        lz0 = mm(lb0, w_ref[0])
        lap1 = share * (lap0 + s0 * lz0) - 2.0 * a0 * s0 * sq0
        lb1 = lap1.astype(BF16)
        lz1 = mm(lb1, w_ref[1])
        lap2 = lap1 + s1 * lz1 - 2.0 * a1 * s1 * sq1
        glz1 = (s1 * gl2).astype(BF16)
        glz0 = (s0 * gl1).astype(BF16)
        gs1 = gl2 * lz1 - cr * x1_ref[...]
        gz1 = (-2.0 * a1 * gs1 + (6.0 * a1 * a1 - 2.0) * gl2 * sq1) * s1
        gz1b = gz1.astype(BF16)
        gw1 = gw_ref[1] + outer(h1_ref[...], gz1b) + outer(lb1, glz1)
        gh1 = mm(gz1b, wt_ref[...])
        gs0 = gl1 * (share * lz0) + x0_ref[...]
        gz0 = (-2.0 * a0 * gs0 + (6.0 * a0 * a0 - 2.0) * gl1 * sq0 + gh1) * s0
        gw0 = gw_ref[0] + outer(hid_ref[...].astype(BF16), gz0.astype(BF16)) + share * outer(lb0, glz0)
        block = width // GROUP
        for y in range(NY):
            for core in range(NC):
                at = (y * NC + core) * block
                base = 2 * block * y
                out_ref[core, base:base + block, :] = gw0[at:at + block]
                out_ref[core, base + block:base + 2 * block, :] = gw1[at:at + block]
        lapsum = jnp.sum(lap2.reshape(walkers, ne, width), axis=1)
        small = []
        for gz in (gz0, gz1):
            for s in range(2):
                small.append(jnp.sum(jnp.where(spin == s, gz, 0.0), axis=0, keepdims=True))
        gread = jnp.zeros((1, width), F32)
        lane = lax.broadcasted_iota(jnp.int32, (1, width), 1)
        energy = jnp.zeros((1, width), F32)
        for i in range(walkers):
            gread -= coeff(i) * (0.5 * lapsum[i:i + 1] + acc_ref[i, 1:2, :])
            e = -0.5 * (jnp.sum(lapsum[i:i + 1] * read, axis=1, keepdims=True) + acc_ref[i, 0:1, :])
            energy = jnp.where(lane == i, e, energy)
        tail = jnp.concatenate(small + [gread, energy, jnp.zeros((2, width), F32)], axis=0)
        for core in range(NC):
            out_ref[core, 2 * block * NY:, :] = tail


def local_part(hidden0, tangent0, laplace0, spins, weights, spin_bias, readout, cot):
    walkers, tangents, ne, width = tangent0.shape
    rows = walkers * ne
    steps = tangents // CHUNK
    body = functools.partial(local_kernel, walkers=walkers, ne=ne, width=width,
                             walkers_all=walkers * NX * NZ)
    full = lambda *shape: pl.BlockSpec(shape, lambda w, k: (0,) * len(shape))
    wide = pltpu.VMEM((rows, width), F32)
    return pl.pallas_call(
        body,
        grid=(walkers, steps),
        out_shape=jax.ShapeDtypeStruct((NC, width + 8, width), F32),
        in_specs=[
            pl.BlockSpec(memory_space=pltpu.SMEM),
            pl.BlockSpec((CHUNK * ne, width), lambda w, k: (w * steps + k, 0)),
            full(rows, width),
            full(rows, width),
            full(rows, 1),
            full(2, width, width),
            full(2, 2, width),
            full(1, width),
        ],
        out_specs=full(NC, width + 8, width),
        scratch_shapes=[pltpu.VMEM((width, width), BF16)] + [wide] * 8 + [pltpu.VMEM((rows, width), BF16)]
        + [wide] * 4 + [pltpu.VMEM((2, width, width), F32), pltpu.VMEM((walkers, 8, width), F32)],
        compiler_params=pltpu.CompilerParams(vmem_limit_bytes=48 * 1024 * 1024),
        name="local_part",
    )(cot, tangent0.reshape(-1, width), hidden0.reshape(rows, width), laplace0.reshape(rows, width),
      spins.reshape(rows, 1), weights, spin_bias, readout.reshape(1, width))


def per_device(hidden0, tangent0, laplace0, spins, weights, spin_bias, readout, energy_cotangent):
    walkers = hidden0.shape[0]
    width = weights.shape[1]
    block = 2 * width // GROUP
    part = local_part(hidden0, tangent0, laplace0, spins, weights, spin_bias, readout, energy_cotangent)
    part = jnp.sum(lax.all_to_all(part, "core", 0, 0), axis=0)
    tail = jnp.broadcast_to(part[None, width:], (NY, 8, width))
    part = jnp.concatenate([part[:width].reshape(NY, block, width), tail], axis=1)
    part = jnp.sum(lax.all_to_all(part, "y", 0, 0), axis=0)
    energy = part[block + 5, :walkers]
    for axis, size in (("x", NX), ("z", NZ)):
        part = jnp.broadcast_to(part[None], (size,) + part.shape)
        part = jnp.sum(lax.all_to_all(part, axis, 0, 0), axis=0)
    grad_weights = part[:block].reshape(2, block // 2, width)
    grad_bias = part[block:block + 4].reshape(2, 2, width)
    return energy, grad_weights, grad_bias, part[block + 4]


def solution(mesh):
    split = Mesh(mesh.devices.reshape(NX, NZ, NY, NC), ("x", "z", "y", "core"))
    walker, tangent = ("x", "z"), ("y", "core")
    in_specs = (
        P(walker, None, None),
        P(walker, tangent, None, None),
        P(walker, None, None),
        P(walker, None),
        P(),
        P(),
        P(),
        P(walker),
    )
    out_specs = (P(walker), P(None, tangent, None), P(), P())
    return jax.shard_map(
        per_device, mesh=split, in_specs=in_specs, out_specs=out_specs, check_vma=False
    )
```

```python
import functools

import jax
import jax.numpy as jnp
from jax import lax
from jax.experimental import pallas as pl
from jax.experimental.pallas import tpu as pltpu
from jax.sharding import Mesh, PartitionSpec as P

NX, NZ, NY, NC = 4, 8, 8, 2
GROUP = NY * NC
CHUNK = 16
F32 = jnp.float32
BF16 = jnp.bfloat16


def mm(a, b):
    return lax.dot_general(a, b, (((1,), (0,)), ((), ())), preferred_element_type=F32)


def outer(a, b):
    return lax.dot_general(a, b, (((0,), (0,)), ((), ())), preferred_element_type=F32)


def local_kernel(cot_ref, tan_ref, hid_ref, lap_ref, spin_ref, w_ref, bias_ref, read_ref, out_ref,
                 wt_ref, a0_ref, a1_ref, s0_ref, s1_ref, amp1_ref, b1_ref, b0_ref, gl1_ref, h1_ref,
                 sq0_ref, sq1_ref, x0_ref, x1_ref, gw_ref, acc_ref, *, walkers, ne, width, walkers_all):
    w = pl.program_id(0)
    k = pl.program_id(1)
    rows = walkers * ne
    read = read_ref[...]

    def coeff(i):
        return cot_ref[i] * (1.0 / walkers_all)

    def spin_column():
        turned = spin_ref[...].astype(F32).T
        return jnp.concatenate([turned[:, i:i + 1] for i in range(walkers)], axis=0)

    @pl.when((w == 0) & (k == 0))
    def _():
        wt_ref[...] = w_ref[1].T
        spin = spin_column()
        hid0 = hid_ref[...]

        def layer(hid, l):
            bias = jnp.where(spin == 0, bias_ref[l, 0:1, :], bias_ref[l, 1:2, :])
            return jnp.tanh(mm(hid.astype(BF16), w_ref[l]) + bias)

        a0 = layer(hid0, 0)
        h1 = hid0 + a0
        a1 = layer(h1, 1)
        a0_ref[...] = a0
        a1_ref[...] = a1
        h1_ref[...] = h1.astype(BF16)
        s0 = 1.0 - a0 * a0
        s1 = 1.0 - a1 * a1
        s0_ref[...] = s0
        s1_ref[...] = s1
        cr = jnp.concatenate([jnp.broadcast_to(coeff(i) * read, (ne, width)) for i in range(walkers)], axis=0)
        gl2 = -0.5 * cr
        amp1_ref[...] = -cr * s1
        b1_ref[...] = 2.0 * cr * a1 * s1
        gl1 = gl2 + mm((s1 * gl2).astype(BF16), wt_ref[...])
        gl1_ref[...] = gl1
        b0_ref[...] = -4.0 * a0 * s0 * gl1
        sq0_ref[...] = jnp.zeros_like(sq0_ref)
        sq1_ref[...] = jnp.zeros_like(sq1_ref)
        x0_ref[...] = jnp.zeros_like(x0_ref)
        x1_ref[...] = jnp.zeros_like(x1_ref)
        gw_ref[...] = jnp.zeros_like(gw_ref)
        acc_ref[...] = jnp.zeros_like(acc_ref)

    c = coeff(w)
    here = pl.ds(pl.multiple_of(w * ne, 8), ne)
    s0 = s0_ref[here]
    s1 = s1_ref[here]
    tan0 = tan_ref[...]

    def split(v):
        return v.reshape(CHUNK, ne, width)

    def flat(v):
        return v.reshape(CHUNK * ne, width)

    z0 = split(mm(tan0, w_ref[0]))
    sq0_ref[here] += jnp.sum(z0 * z0, axis=0)
    tan1 = flat(split(tan0.astype(F32)) + s0[None] * z0).astype(BF16)
    z1 = split(mm(tan1, w_ref[1]))
    sq1_ref[here] += jnp.sum(z1 * z1, axis=0)
    tan2 = split(tan1.astype(F32)) + s1[None] * z1
    tan2 = tan2.astype(BF16).astype(F32)
    cols = jnp.sum(tan2, axis=1)
    g = jnp.sum(cols * read, axis=1, keepdims=True)
    acc_ref[pl.ds(w, 1), 0:1, :] += jnp.broadcast_to(jnp.sum(g * g, axis=0, keepdims=True), (1, width))[None]
    acc_ref[pl.ds(w, 1), 1:2, :] += jnp.sum(g * cols, axis=0, keepdims=True)[None]
    gt = g[:, :, None]
    x1_ref[here] += jnp.sum(gt * z1, axis=0)
    gz1 = flat(gt * amp1_ref[here][None] + b1_ref[here][None] * z1).astype(BF16)
    gw_ref[1] += outer(tan1, gz1)
    gt1 = split(mm(gz1, wt_ref[...])) - (c * gt) * read[None]
    x0_ref[here] += jnp.sum(gt1 * z0, axis=0)
    gz0 = flat(s0[None] * gt1 + b0_ref[here][None] * z0).astype(BF16)
    gw_ref[0] += outer(tan0, gz0)

    @pl.when((w == pl.num_programs(0) - 1) & (k == pl.num_programs(1) - 1))
    def _():
        share = 1.0 / GROUP
        spin = spin_column()
        cr = jnp.concatenate([jnp.broadcast_to(coeff(i) * read, (ne, width)) for i in range(walkers)], axis=0)
        gl2 = -0.5 * cr
        a0, a1, s0, s1, gl1 = a0_ref[...], a1_ref[...], s0_ref[...], s1_ref[...], gl1_ref[...]
        sq0, sq1 = sq0_ref[...], sq1_ref[...]
        lap0 = lap_ref[...]
        lb0 = lap0.astype(BF16)
        lz0 = mm(lb0, w_ref[0])
        lap1 = share * (lap0 + s0 * lz0) - 2.0 * a0 * s0 * sq0
        lb1 = lap1.astype(BF16)
        lz1 = mm(lb1, w_ref[1])
        lap2 = lap1 + s1 * lz1 - 2.0 * a1 * s1 * sq1
        glz1 = (s1 * gl2).astype(BF16)
        glz0 = (s0 * gl1).astype(BF16)
        gs1 = gl2 * lz1 - cr * x1_ref[...]
        gz1 = (-2.0 * a1 * gs1 + (6.0 * a1 * a1 - 2.0) * gl2 * sq1) * s1
        gz1b = gz1.astype(BF16)
        gw1 = gw_ref[1] + outer(h1_ref[...], gz1b) + outer(lb1, glz1)
        gh1 = mm(gz1b, wt_ref[...])
        gs0 = gl1 * (share * lz0) + x0_ref[...]
        gz0 = (-2.0 * a0 * gs0 + (6.0 * a0 * a0 - 2.0) * gl1 * sq0 + gh1) * s0
        gw0 = gw_ref[0] + outer(hid_ref[...].astype(BF16), gz0.astype(BF16)) + share * outer(lb0, glz0)
        block = width // GROUP
        for y in range(NY):
            for core in range(NC):
                at = (y * NC + core) * block
                base = 2 * block * y
                out_ref[core, base:base + block, :] = gw0[at:at + block]
                out_ref[core, base + block:base + 2 * block, :] = gw1[at:at + block]
        lapsum = jnp.sum(lap2.reshape(walkers, ne, width), axis=1)
        small = []
        for gz in (gz0, gz1):
            for s in range(2):
                small.append(jnp.sum(jnp.where(spin == s, gz, 0.0), axis=0, keepdims=True))
        gread = jnp.zeros((1, width), F32)
        lane = lax.broadcasted_iota(jnp.int32, (1, width), 1)
        energy = jnp.zeros((1, width), F32)
        for i in range(walkers):
            gread -= coeff(i) * (0.5 * lapsum[i:i + 1] + acc_ref[i, 1:2, :])
            e = -0.5 * (jnp.sum(lapsum[i:i + 1] * read, axis=1, keepdims=True) + acc_ref[i, 0:1, :])
            energy = jnp.where(lane == i, e, energy)
        tail = jnp.concatenate(small + [gread, energy, jnp.zeros((2, width), F32)], axis=0)
        for core in range(NC):
            out_ref[core, 2 * block * NY:, :] = tail


def local_part(hidden0, tangent0, laplace0, spins, weights, spin_bias, readout, cot):
    walkers, tangents, ne, width = tangent0.shape
    rows = walkers * ne
    steps = tangents // CHUNK
    body = functools.partial(local_kernel, walkers=walkers, ne=ne, width=width,
                             walkers_all=walkers * NX * NZ)
    full = lambda *shape: pl.BlockSpec(shape, lambda w, k: (0,) * len(shape))
    wide = pltpu.VMEM((rows, width), F32)
    return pl.pallas_call(
        body,
        grid=(walkers, steps),
        out_shape=jax.ShapeDtypeStruct((NC, width + 8, width), F32),
        in_specs=[
            pl.BlockSpec(memory_space=pltpu.SMEM),
            pl.BlockSpec((CHUNK * ne, width), lambda w, k: (w * steps + k, 0)),
            full(rows, width),
            full(rows, width),
            full(walkers, ne),
            full(2, width, width),
            full(2, 2, width),
            full(1, width),
        ],
        out_specs=full(NC, width + 8, width),
        scratch_shapes=[pltpu.VMEM((width, width), BF16)] + [wide] * 8 + [pltpu.VMEM((rows, width), BF16)]
        + [wide] * 4 + [pltpu.VMEM((2, width, width), F32), pltpu.VMEM((walkers, 8, width), F32)],
        compiler_params=pltpu.CompilerParams(vmem_limit_bytes=60 * 1024 * 1024),
        name="local_part",
    )(cot, tangent0.reshape(-1, width), hidden0.reshape(rows, width), laplace0.reshape(rows, width),
      spins, weights, spin_bias, readout.reshape(1, width))


def last_sum_kernel(parts_ref, own_ref, energy_ref, weights_ref, bias_ref, read_ref):
    total = jnp.sum(parts_ref[...], axis=0)
    block = weights_ref.shape[1]
    for l in range(2):
        weights_ref[l] = total[l * block:(l + 1) * block]
        bias_ref[l] = total[2 * (block + l):2 * (block + l) + 2]
    read_ref[...] = total[2 * block + 4]
    energy_ref[...] = own_ref[2 * block + 5, :energy_ref.shape[0]]


def last_sum(parts, own, walkers):
    width = parts.shape[-1]
    shapes = ((walkers,), (2, width // GROUP, width), (2, 2, width), (width,))
    return pl.pallas_call(
        last_sum_kernel,
        out_shape=[jax.ShapeDtypeStruct(s, F32) for s in shapes],
        name="last_sum",
    )(parts, own)


def per_device(hidden0, tangent0, laplace0, spins, weights, spin_bias, readout, energy_cotangent):
    walkers = hidden0.shape[0]
    width = weights.shape[1]
    block = 2 * width // GROUP
    part = local_part(hidden0, tangent0, laplace0, spins, weights, spin_bias, readout, energy_cotangent)
    part = jnp.sum(lax.all_to_all(part, "core", 0, 0), axis=0)
    tail = jnp.broadcast_to(part[None, width:], (NY, 8, width))
    part = jnp.concatenate([part[:width].reshape(NY, block, width), tail], axis=1)
    part = jnp.sum(lax.all_to_all(part, "y", 0, 0), axis=0)
    own = part
    part = jnp.broadcast_to(part[None], (NX,) + part.shape)
    part = jnp.sum(lax.all_to_all(part, "x", 0, 0), axis=0)
    part = jnp.broadcast_to(part[None], (NZ,) + part.shape)
    return last_sum(lax.all_to_all(part, "z", 0, 0), own, walkers)


def solution(mesh):
    split = Mesh(mesh.devices.reshape(NX, NZ, NY, NC), ("x", "z", "y", "core"))
    walker, tangent = ("x", "z"), ("y", "core")
    in_specs = (
        P(walker, None, None),
        P(walker, tangent, None, None),
        P(walker, None, None),
        P(walker, None),
        P(),
        P(),
        P(),
        P(walker),
    )
    out_specs = (P(walker), P(None, tangent, None), P(), P())
    return jax.shard_map(
        per_device, mesh=split, in_specs=in_specs, out_specs=out_specs, check_vma=False
    )
```

```python
import functools

import jax
import jax.numpy as jnp
from jax import lax
from jax.experimental import pallas as pl
from jax.experimental.pallas import tpu as pltpu
from jax.sharding import Mesh, PartitionSpec as P

SUBS, SKEW, FINE, VLIM = 4, 1, 1, 60
NX, NZ, NY, NC = 4, 8, 8, 2
GROUP = NY * NC
F32 = jnp.float32
BF16 = jnp.bfloat16


def mm(a, b):
    return lax.dot_general(a, b, (((1,), (0,)), ((), ())), preferred_element_type=F32)


def outer(a, b):
    return lax.dot_general(a, b, (((0,), (0,)), ((), ())), preferred_element_type=F32)


def local_kernel(cot_ref, tan_ref, hid_ref, lap_ref, spin_ref, w_ref, bias_ref, read_ref, mine_ref, theirs_ref,
                 wt_ref, a0_ref, a1_ref, gl1_ref, h1_ref, s0_ref, s1_ref, amp1_ref, b1_ref, b0_ref,
                 sq0_ref, sq1_ref, x0_ref, x1_ref, gw_ref, acc_ref, *, walkers, tangents, ne, width, walkers_all):
    two = 2 * ne
    lo = ne // 16 * 16
    read = read_ref[...]

    def coeff(i):
        return cot_ref[i] * (1.0 / walkers_all)

    def spin_column():
        turned = spin_ref[...].astype(F32).T
        return jnp.concatenate([turned[:, i:i + 1] for i in range(walkers)], axis=0)

    def coeff_rows():
        return jnp.concatenate([jnp.broadcast_to(coeff(i) * read, (ne, width)) for i in range(walkers)], axis=0)

    wt_ref[...] = w_ref[1].T
    spin = spin_column()
    hid0 = hid_ref[...]

    def layer(hid, l):
        bias = jnp.where(spin == 0, bias_ref[l, 0:1, :], bias_ref[l, 1:2, :])
        return jnp.tanh(mm(hid.astype(BF16), w_ref[l]) + bias)

    def keep_twice(ref, v):
        for i in range(walkers):
            one = v[i * ne:(i + 1) * ne]
            ref[i] = jnp.concatenate([one, one], axis=0).astype(BF16)

    a0 = layer(hid0, 0)
    h1 = hid0 + a0
    a1 = layer(h1, 1)
    a0_ref[...] = a0
    a1_ref[...] = a1
    h1_ref[...] = h1.astype(BF16)
    s0 = 1.0 - a0 * a0
    s1 = 1.0 - a1 * a1
    cr = coeff_rows()
    gl2 = -0.5 * cr
    gl1 = gl2 + mm((s1 * gl2).astype(BF16), wt_ref[...])
    gl1_ref[...] = gl1
    keep_twice(s0_ref, s0)
    keep_twice(s1_ref, s1)
    keep_twice(amp1_ref, -cr * s1)
    keep_twice(b1_ref, 2.0 * cr * a1 * s1)
    keep_twice(b0_ref, -4.0 * a0 * s0 * gl1)
    gw_ref[...] = jnp.zeros_like(gw_ref)

    tangents_u = tangents // SUBS
    pairs = tangents_u // 2
    span = tangents_u * ne
    units = [(w, p) for w in range(walkers) for p in range(SUBS)]

    def split(v):
        return v.reshape(pairs, two, width)

    def flat(v):
        return v.reshape(pairs * two, width)

    def fold(v):
        half = v[:pairs // 2] + v[pairs // 2:]
        total = jnp.sum(half.astype(F32), axis=0)
        return total[:ne] + total[ne:]

    def rows_of(p, v):
        a = jnp.broadcast_to(v[2 * p:2 * p + 1], (lo, width)).astype(BF16)
        b = jnp.broadcast_to(v[2 * p + 1:2 * p + 2], (two - lo - 16, width)).astype(BF16)
        mid = jnp.concatenate([jnp.broadcast_to(v[2 * p:2 * p + 1], (ne - lo, width)),
                               jnp.broadcast_to(v[2 * p + 1:2 * p + 2], (16 - ne + lo, width))], axis=0)
        return jnp.concatenate([a, mid.astype(BF16), b], axis=0)

    def add(u, ref, v):
        w, p = units[u]
        ref[w] = v if p == 0 else ref[w] + v

    def tan0_of(u):
        return tan_ref[u * span:(u + 1) * span, :]

    n = len(units)
    z0, tan1, z1, gb, gz1, back, gz0 = ([None] * n for _ in range(7))

    def start(u):
        z0[u] = split(mm(tan0_of(u), w_ref[0]).astype(BF16))

    def first(u):
        w = units[u][0]
        add(u, sq0_ref, fold(z0[u] * z0[u]))
        tan1[u] = split(tan0_of(u)) + s0_ref[w][None] * z0[u]

    def second(u):
        z1[u] = split(mm(flat(tan1[u]), w_ref[1]).astype(BF16))

    def third(u):
        w = units[u][0]
        add(u, sq1_ref, fold(z1[u] * z1[u]))
        tan2 = tan1[u] + s1_ref[w][None] * z1[u]
        cols = jnp.sum(flat(tan2).astype(F32).reshape(tangents_u, ne, width), axis=1)
        g = jnp.sum(cols * read, axis=1, keepdims=True)
        squares = jnp.broadcast_to(jnp.sum(g * g, axis=0, keepdims=True), (1, width))
        add(u, acc_ref, jnp.concatenate([squares, jnp.sum(g * cols, axis=0, keepdims=True)], axis=0))
        gb[u] = jnp.broadcast_to(g, (tangents_u, width))

    def fourth(u):
        w = units[u][0]
        gains = jnp.stack([rows_of(p, gb[u]) for p in range(pairs)])
        add(u, x1_ref, fold(gains * z1[u]))
        gz1[u] = flat(gains * amp1_ref[w][None] + b1_ref[w][None] * z1[u])

    def fifth(u):
        back[u] = split(mm(gz1[u], wt_ref[...]).astype(BF16))

    def outer1(u):
        gw_ref[1] += outer(flat(tan1[u]), gz1[u])

    def sixth(u):
        w = units[u][0]
        pull = gb[u] * (-coeff(w) * read)
        gt1 = back[u] + jnp.stack([rows_of(p, pull) for p in range(pairs)])
        add(u, x0_ref, fold(gt1 * z0[u]))
        gz0[u] = flat(s0_ref[w][None] * gt1 + b0_ref[w][None] * z0[u])

    def outer0(u):
        gw_ref[0] += outer(tan0_of(u), gz0[u])

    stages = [(start,), (first, second), (third, fourth, fifth), (outer1, sixth), (outer0,)]
    if FINE:
        stages = [(start,), (first,), (second,), (third,), (fourth,), (fifth, outer1), (sixth,), (outer0,)]
    if SKEW:
        for tick in range(n + len(stages) - 1):
            for k in reversed(range(len(stages))):
                if 0 <= tick - k < n:
                    for f in stages[k]:
                        f(tick - k)
    else:
        for stage in stages:
            for u in range(n):
                for f in stage:
                    f(u)

    share = 1.0 / GROUP
    spin = spin_column()
    cr = coeff_rows()
    gl2 = -0.5 * cr
    a0, a1, gl1 = a0_ref[...], a1_ref[...], gl1_ref[...]
    s0 = 1.0 - a0 * a0
    s1 = 1.0 - a1 * a1
    whole = lambda ref: ref[...].reshape(walkers * ne, width)
    sq0, sq1 = whole(sq0_ref), whole(sq1_ref)
    lap0 = lap_ref[...]
    lb0 = lap0.astype(BF16)
    lz0 = mm(lb0, w_ref[0])
    lap1 = share * (lap0 + s0 * lz0) - 2.0 * a0 * s0 * sq0
    lb1 = lap1.astype(BF16)
    lz1 = mm(lb1, w_ref[1])
    lap2 = lap1 + s1 * lz1 - 2.0 * a1 * s1 * sq1
    glz1 = (s1 * gl2).astype(BF16)
    glz0 = (s0 * gl1).astype(BF16)
    gs1 = gl2 * lz1 - cr * whole(x1_ref)
    gz1 = (-2.0 * a1 * gs1 + (6.0 * a1 * a1 - 2.0) * gl2 * sq1) * s1
    gz1b = gz1.astype(BF16)
    gw_ref[1] += outer(h1_ref[...], gz1b) + outer(lb1, glz1)
    gh1 = mm(gz1b, wt_ref[...])
    gs0 = gl1 * (share * lz0) + whole(x0_ref)
    gz0 = (-2.0 * a0 * gs0 + (6.0 * a0 * a0 - 2.0) * gl1 * sq0 + gh1) * s0
    gw_ref[0] += outer(hid_ref[...].astype(BF16), gz0.astype(BF16)) + share * outer(lb0, glz0)
    lapsum = jnp.sum(lap2.reshape(walkers, ne, width), axis=1)
    small = []
    for gz in (gz0, gz1):
        for s in range(2):
            small.append(jnp.sum(jnp.where(spin == s, gz, 0.0), axis=0, keepdims=True))
    gread = jnp.zeros((1, width), F32)
    lane = lax.broadcasted_iota(jnp.int32, (1, width), 1)
    energy = jnp.zeros((1, width), F32)
    for i in range(walkers):
        gread -= coeff(i) * (0.5 * lapsum[i:i + 1] + acc_ref[i, 1:2, :])
        e = -0.5 * (jnp.sum(lapsum[i:i + 1] * read, axis=1, keepdims=True) + acc_ref[i, 0:1, :])
        energy = jnp.where(lane == i, e, energy)
    tail = jnp.concatenate(small + [gread, energy, jnp.zeros((2, width), F32)], axis=0)
    block = width // GROUP
    own = core_index()
    for ref, core in ((mine_ref, own), (theirs_ref, 1 - own)):
        for y in range(NY):
            at = pl.multiple_of((y * NC + core) * block, block)
            for l in range(2):
                ref[y, l * block:(l + 1) * block, :] = gw_ref[l, pl.ds(at, block), :]
            ref[y, 2 * block:, :] = tail


def core_index():
    return lax.axis_index("core")


def local_part(hidden0, tangent0, laplace0, spins, weights, spin_bias, readout, cot):
    walkers, tangents, ne, width = tangent0.shape
    rows = walkers * ne
    half = (NY, 2 * width // GROUP + 8, width)
    body = functools.partial(local_kernel, walkers=walkers, tangents=tangents, ne=ne, width=width,
                             walkers_all=walkers * NX * NZ)
    full = lambda *shape: pl.BlockSpec(shape, lambda w: (0,) * len(shape))
    wide = pltpu.VMEM((rows, width), F32)
    twice = pltpu.VMEM((walkers, 2 * ne, width), BF16)
    sums = pltpu.VMEM((walkers, ne, width), F32)
    return pl.pallas_call(
        body,
        grid=(1,),
        out_shape=[jax.ShapeDtypeStruct(half, F32)] * 2,
        in_specs=[
            pl.BlockSpec(memory_space=pltpu.SMEM),
            full(walkers * tangents * ne, width),
            full(rows, width),
            full(rows, width),
            full(walkers, ne),
            full(2, width, width),
            full(2, 2, width),
            full(1, width),
        ],
        out_specs=[full(*half)] * 2,
        scratch_shapes=[pltpu.VMEM((width, width), BF16)] + [wide] * 3 + [pltpu.VMEM((rows, width), BF16)]
        + [twice] * 5 + [sums] * 4 + [pltpu.VMEM((2, width, width), F32), pltpu.VMEM((walkers, 2, width), F32)],
        compiler_params=pltpu.CompilerParams(vmem_limit_bytes=VLIM * 1024 * 1024),
        name="local_part",
    )(cot, tangent0.reshape(-1, width), hidden0.reshape(rows, width), laplace0.reshape(rows, width),
      spins, weights, spin_bias, readout.reshape(1, width))


def last_sum_kernel(parts_ref, own_ref, energy_ref, weights_ref, bias_ref, read_ref):
    total = jnp.sum(parts_ref[...], axis=0)
    block = weights_ref.shape[1]
    for l in range(2):
        weights_ref[l] = total[l * block:(l + 1) * block]
        bias_ref[l] = total[2 * (block + l):2 * (block + l) + 2]
    read_ref[...] = total[2 * block + 4]
    energy_ref[...] = own_ref[2 * block + 5, :energy_ref.shape[0]]


def last_sum(parts, own, walkers):
    width = parts.shape[-1]
    shapes = ((walkers,), (2, width // GROUP, width), (2, 2, width), (width,))
    return pl.pallas_call(
        last_sum_kernel,
        out_shape=[jax.ShapeDtypeStruct(s, F32) for s in shapes],
        name="last_sum",
    )(parts, own)


def per_device(hidden0, tangent0, laplace0, spins, weights, spin_bias, readout, energy_cotangent):
    walkers = hidden0.shape[0]
    width = weights.shape[1]
    mine, theirs = local_part(hidden0, tangent0, laplace0, spins, weights, spin_bias, readout, energy_cotangent)
    part = mine + lax.ppermute(theirs, "core", [(0, 1), (1, 0)])
    part = jnp.sum(lax.all_to_all(part, "y", 0, 0), axis=0)
    own = part
    part = jnp.broadcast_to(part[None], (NX,) + part.shape)
    part = jnp.sum(lax.all_to_all(part, "x", 0, 0), axis=0)
    part = jnp.broadcast_to(part[None], (NZ,) + part.shape)
    return last_sum(lax.all_to_all(part, "z", 0, 0), own, walkers)


def solution(mesh):
    split = Mesh(mesh.devices.reshape(NX, NZ, NY, NC), ("x", "z", "y", "core"))
    walker, tangent = ("x", "z"), ("y", "core")
    in_specs = (
        P(walker, None, None),
        P(walker, tangent, None, None),
        P(walker, None, None),
        P(walker, None),
        P(),
        P(),
        P(),
        P(walker),
    )
    out_specs = (P(walker), P(None, tangent, None), P(), P())
    return jax.shard_map(
        per_device, mesh=split, in_specs=in_specs, out_specs=out_specs, check_vma=False
    )
```

```python
import functools

import jax
import jax.numpy as jnp
from jax import lax
from jax.experimental import pallas as pl
from jax.experimental.pallas import tpu as pltpu
from jax.sharding import Mesh, PartitionSpec as P

SUBS, SKEW, FINE, VLIM = 4, 1, 1, 60
NX, NZ, NY, NC = 4, 8, 8, 2
GROUP = NY * NC
LANES, HALF = 128, 64
PIECE = 19
F32 = jnp.float32
BF16 = jnp.bfloat16


def mm(a, b):
    return lax.dot_general(a, b, (((1,), (0,)), ((), ())), preferred_element_type=F32)


def outer(a, b):
    return lax.dot_general(a, b, (((0,), (0,)), ((), ())), preferred_element_type=F32)


def local_kernel(cot_ref, tan_ref, hid_ref, lap_ref, spin_ref, w_ref, bias_ref, read_ref, mine_ref, theirs_ref,
                 wt_ref, a0_ref, a1_ref, gl1_ref, h1_ref, s0_ref, s1_ref, amp1_ref, b1_ref, b0_ref,
                 sq0_ref, sq1_ref, x0_ref, x1_ref, gw_ref, acc_ref, *, walkers, tangents, ne, width, walkers_all):
    two = 2 * ne
    lo = ne // 16 * 16
    read = read_ref[...]

    def coeff(i):
        return cot_ref[i] * (1.0 / walkers_all)

    def spin_column():
        turned = spin_ref[...].astype(F32).T
        return jnp.concatenate([turned[:, i:i + 1] for i in range(walkers)], axis=0)

    def coeff_rows():
        return jnp.concatenate([jnp.broadcast_to(coeff(i) * read, (ne, width)) for i in range(walkers)], axis=0)

    wt_ref[...] = w_ref[1].T
    spin = spin_column()
    hid0 = hid_ref[...]

    def layer(hid, l):
        bias = jnp.where(spin == 0, bias_ref[l, 0:1, :], bias_ref[l, 1:2, :])
        return jnp.tanh(mm(hid.astype(BF16), w_ref[l]) + bias)

    def keep_twice(ref, v):
        for i in range(walkers):
            one = v[i * ne:(i + 1) * ne]
            ref[i] = jnp.concatenate([one, one], axis=0).astype(BF16)

    a0 = layer(hid0, 0)
    h1 = hid0 + a0
    a1 = layer(h1, 1)
    a0_ref[...] = a0
    a1_ref[...] = a1
    h1_ref[...] = h1.astype(BF16)
    s0 = 1.0 - a0 * a0
    s1 = 1.0 - a1 * a1
    cr = coeff_rows()
    gl2 = -0.5 * cr
    gl1 = gl2 + mm((s1 * gl2).astype(BF16), wt_ref[...])
    gl1_ref[...] = gl1
    keep_twice(s0_ref, s0)
    keep_twice(s1_ref, s1)
    keep_twice(amp1_ref, -cr * s1)
    keep_twice(b1_ref, 2.0 * cr * a1 * s1)
    keep_twice(b0_ref, -4.0 * a0 * s0 * gl1)
    gw_ref[...] = jnp.zeros_like(gw_ref)

    tangents_u = tangents // SUBS
    pairs = tangents_u // 2
    span = tangents_u * ne
    units = [(w, p) for w in range(walkers) for p in range(SUBS)]

    def split(v):
        return v.reshape(pairs, two, width)

    def flat(v):
        return v.reshape(pairs * two, width)

    def fold(v):
        half = v[:pairs // 2] + v[pairs // 2:]
        total = jnp.sum(half.astype(F32), axis=0)
        return total[:ne] + total[ne:]

    def rows_of(p, v):
        a = jnp.broadcast_to(v[2 * p:2 * p + 1], (lo, width)).astype(BF16)
        b = jnp.broadcast_to(v[2 * p + 1:2 * p + 2], (two - lo - 16, width)).astype(BF16)
        mid = jnp.concatenate([jnp.broadcast_to(v[2 * p:2 * p + 1], (ne - lo, width)),
                               jnp.broadcast_to(v[2 * p + 1:2 * p + 2], (16 - ne + lo, width))], axis=0)
        return jnp.concatenate([a, mid.astype(BF16), b], axis=0)

    def add(u, ref, v):
        w, p = units[u]
        ref[w] = v if p == 0 else ref[w] + v

    def tan0_of(u):
        return tan_ref[u * span:(u + 1) * span, :]

    n = len(units)
    z0, tan1, z1, gb, gz1, back, gz0 = ([None] * n for _ in range(7))

    def start(u):
        z0[u] = split(mm(tan0_of(u), w_ref[0]).astype(BF16))

    def first(u):
        w = units[u][0]
        add(u, sq0_ref, fold(z0[u] * z0[u]))
        tan1[u] = split(tan0_of(u)) + s0_ref[w][None] * z0[u]

    def second(u):
        z1[u] = split(mm(flat(tan1[u]), w_ref[1]).astype(BF16))

    def third(u):
        w = units[u][0]
        add(u, sq1_ref, fold(z1[u] * z1[u]))
        tan2 = tan1[u] + s1_ref[w][None] * z1[u]
        cols = jnp.sum(flat(tan2).astype(F32).reshape(tangents_u, ne, width), axis=1)
        g = jnp.sum(cols * read, axis=1, keepdims=True)
        squares = jnp.broadcast_to(jnp.sum(g * g, axis=0, keepdims=True), (1, width))
        add(u, acc_ref, jnp.concatenate([squares, jnp.sum(g * cols, axis=0, keepdims=True)], axis=0))
        gb[u] = jnp.broadcast_to(g, (tangents_u, width))

    def fourth(u):
        w = units[u][0]
        gains = jnp.stack([rows_of(p, gb[u]) for p in range(pairs)])
        add(u, x1_ref, fold(gains * z1[u]))
        gz1[u] = flat(gains * amp1_ref[w][None] + b1_ref[w][None] * z1[u])

    def fifth(u):
        back[u] = split(mm(gz1[u], wt_ref[...]).astype(BF16))

    def outer1(u):
        gw_ref[1] += outer(flat(tan1[u]), gz1[u])

    def sixth(u):
        w = units[u][0]
        pull = gb[u] * (-coeff(w) * read)
        gt1 = back[u] + jnp.stack([rows_of(p, pull) for p in range(pairs)])
        add(u, x0_ref, fold(gt1 * z0[u]))
        gz0[u] = flat(s0_ref[w][None] * gt1 + b0_ref[w][None] * z0[u])

    def outer0(u):
        gw_ref[0] += outer(tan0_of(u), gz0[u])

    stages = [(start,), (first, second), (third, fourth, fifth), (outer1, sixth), (outer0,)]
    if FINE:
        stages = [(start,), (first,), (second,), (third,), (fourth,), (fifth, outer1), (sixth,), (outer0,)]
    if SKEW:
        for tick in range(n + len(stages) - 1):
            for k in reversed(range(len(stages))):
                if 0 <= tick - k < n:
                    for f in stages[k]:
                        f(tick - k)
    else:
        for stage in stages:
            for u in range(n):
                for f in stage:
                    f(u)

    share = 1.0 / GROUP
    spin = spin_column()
    cr = coeff_rows()
    gl2 = -0.5 * cr
    a0, a1, gl1 = a0_ref[...], a1_ref[...], gl1_ref[...]
    s0 = 1.0 - a0 * a0
    s1 = 1.0 - a1 * a1
    whole = lambda ref: ref[...].reshape(walkers * ne, width)
    sq0, sq1 = whole(sq0_ref), whole(sq1_ref)
    lap0 = lap_ref[...]
    lb0 = lap0.astype(BF16)
    lz0 = mm(lb0, w_ref[0])
    lap1 = share * (lap0 + s0 * lz0) - 2.0 * a0 * s0 * sq0
    lb1 = lap1.astype(BF16)
    lz1 = mm(lb1, w_ref[1])
    lap2 = lap1 + s1 * lz1 - 2.0 * a1 * s1 * sq1
    glz1 = (s1 * gl2).astype(BF16)
    glz0 = (s0 * gl1).astype(BF16)
    gs1 = gl2 * lz1 - cr * whole(x1_ref)
    gz1 = (-2.0 * a1 * gs1 + (6.0 * a1 * a1 - 2.0) * gl2 * sq1) * s1
    gz1b = gz1.astype(BF16)
    gw_ref[1] += outer(h1_ref[...], gz1b) + outer(lb1, glz1)
    gh1 = mm(gz1b, wt_ref[...])
    gs0 = gl1 * (share * lz0) + whole(x0_ref)
    gz0 = (-2.0 * a0 * gs0 + (6.0 * a0 * a0 - 2.0) * gl1 * sq0 + gh1) * s0
    gw_ref[0] += outer(hid_ref[...].astype(BF16), gz0.astype(BF16)) + share * outer(lb0, glz0)
    lapsum = jnp.sum(lap2.reshape(walkers, ne, width), axis=1)
    small = []
    for gz in (gz0, gz1):
        for s in range(2):
            small.append(jnp.sum(jnp.where(spin == s, gz, 0.0), axis=0, keepdims=True))
    gread = jnp.zeros((1, width), F32)
    energy = []
    for i in range(walkers):
        gread -= coeff(i) * (0.5 * lapsum[i:i + 1] + acc_ref[i, 1:2, :])
        energy.append(-0.5 * (jnp.sum(lapsum[i:i + 1] * read, axis=1, keepdims=True) + acc_ref[i, 0:1, 0:1]))
    lane = lax.broadcasted_iota(jnp.int32, (1, LANES), 1)
    here = HALF + walkers * x_index()
    slots = jnp.zeros((1, LANES), F32)
    for i in range(walkers):
        slots = jnp.where(lane == here + i, energy[i], slots)
    extras = [small_part(small + [gread], q, slots, lane) for q in range(NX)]
    block = width // GROUP
    own = core_index()
    for ref, core, sign in ((mine_ref, own, -1.0), (theirs_ref, 1 - own, 1.0)):
        for y in range(NY):
            at = pl.multiple_of((y * NC + core) * block, block)
            for q in range(NX):
                l, sub = divmod(q, 2)
                rows_q = sign * gw_ref[l, pl.ds(at + 8 * sub, 8), :]
                base = PIECE * (y * NX + q)
                ref[base:base + 8, :] = rows_q[:, :LANES]
                ref[base + 8:base + 16, :] = rows_q[:, LANES:]
                ref[base + 16:base + PIECE, :] = sign * extras[q]


def small_part(small, q, slots, lane):
    half, sub = divmod(q, 2)

    def low(r):
        v = small[r][:, half * LANES:(half + 1) * LANES]
        return pltpu.roll(v, HALF, 1) if sub else v

    def high(r):
        v = small[r][:, half * LANES:(half + 1) * LANES]
        return v if sub else pltpu.roll(v, HALF, 1)

    first = lane < HALF
    return jnp.concatenate([jnp.where(first, low(0), high(1)), jnp.where(first, low(2), high(3)),
                            jnp.where(first, low(4), slots)], axis=0)


def x_index():
    return lax.axis_index("x")


def core_index():
    return lax.axis_index("core")


def local_part(hidden0, tangent0, laplace0, spins, weights, spin_bias, readout, cot):
    walkers, tangents, ne, width = tangent0.shape
    rows = walkers * ne
    half = (NY * NX * PIECE, LANES)
    body = functools.partial(local_kernel, walkers=walkers, tangents=tangents, ne=ne, width=width,
                             walkers_all=walkers * NX * NZ)
    full = lambda *shape: pl.BlockSpec(shape, lambda w: (0,) * len(shape))
    wide = pltpu.VMEM((rows, width), F32)
    twice = pltpu.VMEM((walkers, 2 * ne, width), BF16)
    sums = pltpu.VMEM((walkers, ne, width), F32)
    return pl.pallas_call(
        body,
        grid=(1,),
        out_shape=[jax.ShapeDtypeStruct(half, F32)] * 2,
        in_specs=[
            pl.BlockSpec(memory_space=pltpu.SMEM),
            full(walkers * tangents * ne, width),
            full(rows, width),
            full(rows, width),
            full(walkers, ne),
            full(2, width, width),
            full(2, 2, width),
            full(1, width),
        ],
        out_specs=[full(*half)] * 2,
        scratch_shapes=[pltpu.VMEM((width, width), BF16)] + [wide] * 3 + [pltpu.VMEM((rows, width), BF16)]
        + [twice] * 5 + [sums] * 4 + [pltpu.VMEM((2, width, width), F32), pltpu.VMEM((walkers, 2, width), F32)],
        compiler_params=pltpu.CompilerParams(vmem_limit_bytes=VLIM * 1024 * 1024),
        name="local_part",
    )(cot, tangent0.reshape(-1, width), hidden0.reshape(rows, width), laplace0.reshape(rows, width),
      spins, weights, spin_bias, readout.reshape(1, width))


def last_sum_kernel(parts_ref, own_ref, energy_ref, weights_ref, bias_ref, read_ref):
    walkers = energy_ref.shape[0]
    totals = []
    for q in range(NX):
        pieces = [parts_ref[PIECE * (q * NZ + z):PIECE * (q * NZ + z + 1), :] for z in range(NZ)]
        total = sum(pieces[1:], pieces[0])
        l, sub = divmod(q, 2)
        weights_ref[l, 8 * sub:8 * sub + 8, :LANES] = total[:8]
        weights_ref[l, 8 * sub:8 * sub + 8, LANES:] = total[8:16]
        totals.append(total[16:])
    lane = lax.broadcasted_iota(jnp.int32, (1, LANES), 1)
    first = lane < HALF

    def small_row(r):
        at = slice(r // 2, r // 2 + 1)
        halves = []
        for half in range(2):
            a, b = totals[2 * half][at], totals[2 * half + 1][at]
            if r % 2 == 0:
                b = pltpu.roll(b, HALF, 1)
            else:
                a = pltpu.roll(a, HALF, 1)
            halves.append(jnp.where(first, a, b))
        return jnp.concatenate(halves, axis=1)

    for l in range(2):
        bias_ref[l] = jnp.concatenate([small_row(2 * l), small_row(2 * l + 1)], axis=0)
    read_ref[...] = small_row(4)[0]
    slots = own_ref[PIECE - 1:PIECE, :]
    here = HALF + walkers * x_index()
    spread = jnp.zeros((1, LANES), F32)
    for i in range(walkers):
        one = jnp.sum(jnp.where(lane == here + i, slots, 0.0), axis=1, keepdims=True)
        spread = jnp.where(lane == i, one, spread)
    energy_ref[...] = spread[0, :walkers]


def last_sum(parts, own, walkers, width):
    shapes = ((walkers,), (2, width // GROUP, width), (2, 2, width), (width,))
    return pl.pallas_call(
        last_sum_kernel,
        out_shape=[jax.ShapeDtypeStruct(s, F32) for s in shapes],
        name="last_sum",
    )(parts.reshape(-1, LANES), own.reshape(PIECE, LANES))


def per_device(hidden0, tangent0, laplace0, spins, weights, spin_bias, readout, energy_cotangent):
    walkers = hidden0.shape[0]
    width = weights.shape[1]
    minus, theirs = local_part(hidden0, tangent0, laplace0, spins, weights, spin_bias, readout, energy_cotangent)
    got = lax.ppermute(theirs, "core", [(0, 1), (1, 0)])
    part = (lax.optimization_barrier(-minus) + got).reshape(NY * NX, PIECE, 1, LANES)
    own = jnp.sum(lax.all_to_all(part, ("y", "x"), 0, 0), axis=0)
    part = jnp.broadcast_to(own[None], (NX * NZ,) + own.shape)
    return last_sum(lax.all_to_all(part, ("x", "z"), 0, 0), own, walkers, width)


def solution(mesh):
    split = Mesh(mesh.devices.reshape(NX, NZ, NY, NC), ("x", "z", "y", "core"))
    walker, tangent = ("x", "z"), ("y", "core")
    in_specs = (
        P(walker, None, None),
        P(walker, tangent, None, None),
        P(walker, None, None),
        P(walker, None),
        P(),
        P(),
        P(),
        P(walker),
    )
    out_specs = (P(walker), P(None, tangent, None), P(), P())
    return jax.shard_map(
        per_device, mesh=split, in_specs=in_specs, out_specs=out_specs, check_vma=False
    )
```

```python
import functools

import jax
import jax.numpy as jnp
from jax import lax
from jax.experimental import pallas as pl
from jax.experimental.pallas import tpu as pltpu
from jax.sharding import Mesh, PartitionSpec as P

SUBS, SKEW, FINE, VLIM = 4, 1, 1, 60
NX, NZ, NY, NC = 4, 8, 8, 2
GROUP = NY * NC
LANES, HALF = 128, 64
PIECE = 19
STRIDE = 3
X_ORDER = (0, 2, 1, 3)
YX_ORDER = [(STRIDE * k % NY, x) for x in X_ORDER for k in range(NY)]
XZ_ORDER = [(x, STRIDE * k % NZ) for x in X_ORDER for k in range(NZ)]
F32 = jnp.float32
BF16 = jnp.bfloat16


def mm(a, b):
    return lax.dot_general(a, b, (((1,), (0,)), ((), ())), preferred_element_type=F32)


def outer(a, b):
    return lax.dot_general(a, b, (((0,), (0,)), ((), ())), preferred_element_type=F32)


def local_kernel(cot_ref, tan_ref, hid_ref, lap_ref, spin_ref, w_ref, bias_ref, read_ref, mine_ref, theirs_ref,
                 wt_ref, a0_ref, a1_ref, gl1_ref, h1_ref, s0_ref, s1_ref, amp1_ref, b1_ref, b0_ref,
                 sq0_ref, sq1_ref, x0_ref, x1_ref, gw_ref, acc_ref, *, walkers, tangents, ne, width, walkers_all):
    two = 2 * ne
    lo = ne // 16 * 16
    read = read_ref[...]

    def coeff(i):
        return cot_ref[i] * (1.0 / walkers_all)

    def spin_column():
        turned = spin_ref[...].astype(F32).T
        return jnp.concatenate([turned[:, i:i + 1] for i in range(walkers)], axis=0)

    def coeff_rows():
        return jnp.concatenate([jnp.broadcast_to(coeff(i) * read, (ne, width)) for i in range(walkers)], axis=0)

    wt_ref[...] = w_ref[1].T
    spin = spin_column()
    hid0 = hid_ref[...]

    def layer(hid, l):
        bias = jnp.where(spin == 0, bias_ref[l, 0:1, :], bias_ref[l, 1:2, :])
        return jnp.tanh(mm(hid.astype(BF16), w_ref[l]) + bias)

    def keep_twice(ref, v):
        for i in range(walkers):
            one = v[i * ne:(i + 1) * ne]
            ref[i] = jnp.concatenate([one, one], axis=0).astype(BF16)

    a0 = layer(hid0, 0)
    h1 = hid0 + a0
    a1 = layer(h1, 1)
    a0_ref[...] = a0
    a1_ref[...] = a1
    h1_ref[...] = h1.astype(BF16)
    s0 = 1.0 - a0 * a0
    s1 = 1.0 - a1 * a1
    cr = coeff_rows()
    gl2 = -0.5 * cr
    gl1 = gl2 + mm((s1 * gl2).astype(BF16), wt_ref[...])
    gl1_ref[...] = gl1
    keep_twice(s0_ref, s0)
    keep_twice(s1_ref, s1)
    keep_twice(amp1_ref, -cr * s1)
    keep_twice(b1_ref, 2.0 * cr * a1 * s1)
    keep_twice(b0_ref, -4.0 * a0 * s0 * gl1)
    gw_ref[...] = jnp.zeros_like(gw_ref)

    tangents_u = tangents // SUBS
    pairs = tangents_u // 2
    span = tangents_u * ne
    units = [(w, p) for w in range(walkers) for p in range(SUBS)]

    def split(v):
        return v.reshape(pairs, two, width)

    def flat(v):
        return v.reshape(pairs * two, width)

    def fold(v):
        half = v[:pairs // 2] + v[pairs // 2:]
        total = jnp.sum(half.astype(F32), axis=0)
        return total[:ne] + total[ne:]

    def rows_of(p, v):
        a = jnp.broadcast_to(v[2 * p:2 * p + 1], (lo, width)).astype(BF16)
        b = jnp.broadcast_to(v[2 * p + 1:2 * p + 2], (two - lo - 16, width)).astype(BF16)
        mid = jnp.concatenate([jnp.broadcast_to(v[2 * p:2 * p + 1], (ne - lo, width)),
                               jnp.broadcast_to(v[2 * p + 1:2 * p + 2], (16 - ne + lo, width))], axis=0)
        return jnp.concatenate([a, mid.astype(BF16), b], axis=0)

    def add(u, ref, v):
        w, p = units[u]
        ref[w] = v if p == 0 else ref[w] + v

    def tan0_of(u):
        return tan_ref[u * span:(u + 1) * span, :]

    n = len(units)
    z0, tan1, z1, gb, gz1, back, gz0 = ([None] * n for _ in range(7))

    def start(u):
        z0[u] = split(mm(tan0_of(u), w_ref[0]).astype(BF16))

    def first(u):
        w = units[u][0]
        add(u, sq0_ref, fold(z0[u] * z0[u]))
        tan1[u] = split(tan0_of(u)) + s0_ref[w][None] * z0[u]

    def second(u):
        z1[u] = split(mm(flat(tan1[u]), w_ref[1]).astype(BF16))

    def third(u):
        w = units[u][0]
        add(u, sq1_ref, fold(z1[u] * z1[u]))
        tan2 = tan1[u] + s1_ref[w][None] * z1[u]
        cols = jnp.sum(flat(tan2).astype(F32).reshape(tangents_u, ne, width), axis=1)
        g = jnp.sum(cols * read, axis=1, keepdims=True)
        squares = jnp.broadcast_to(jnp.sum(g * g, axis=0, keepdims=True), (1, width))
        add(u, acc_ref, jnp.concatenate([squares, jnp.sum(g * cols, axis=0, keepdims=True)], axis=0))
        gb[u] = jnp.broadcast_to(g, (tangents_u, width))

    def fourth(u):
        w = units[u][0]
        gains = jnp.stack([rows_of(p, gb[u]) for p in range(pairs)])
        add(u, x1_ref, fold(gains * z1[u]))
        gz1[u] = flat(gains * amp1_ref[w][None] + b1_ref[w][None] * z1[u])

    def fifth(u):
        back[u] = split(mm(gz1[u], wt_ref[...]).astype(BF16))

    def outer1(u):
        gw_ref[1] += outer(flat(tan1[u]), gz1[u])

    def sixth(u):
        w = units[u][0]
        pull = gb[u] * (-coeff(w) * read)
        gt1 = back[u] + jnp.stack([rows_of(p, pull) for p in range(pairs)])
        add(u, x0_ref, fold(gt1 * z0[u]))
        gz0[u] = flat(s0_ref[w][None] * gt1 + b0_ref[w][None] * z0[u])

    def outer0(u):
        gw_ref[0] += outer(tan0_of(u), gz0[u])

    stages = [(start,), (first, second), (third, fourth, fifth), (outer1, sixth), (outer0,)]
    if FINE:
        stages = [(start,), (first,), (second,), (third,), (fourth,), (fifth, outer1), (sixth,), (outer0,)]
    if SKEW:
        for tick in range(n + len(stages) - 1):
            for k in reversed(range(len(stages))):
                if 0 <= tick - k < n:
                    for f in stages[k]:
                        f(tick - k)
    else:
        for stage in stages:
            for u in range(n):
                for f in stage:
                    f(u)

    share = 1.0 / GROUP
    spin = spin_column()
    cr = coeff_rows()
    gl2 = -0.5 * cr
    a0, a1, gl1 = a0_ref[...], a1_ref[...], gl1_ref[...]
    s0 = 1.0 - a0 * a0
    s1 = 1.0 - a1 * a1
    whole = lambda ref: ref[...].reshape(walkers * ne, width)
    sq0, sq1 = whole(sq0_ref), whole(sq1_ref)
    lap0 = lap_ref[...]
    lb0 = lap0.astype(BF16)
    lz0 = mm(lb0, w_ref[0])
    lap1 = share * (lap0 + s0 * lz0) - 2.0 * a0 * s0 * sq0
    lb1 = lap1.astype(BF16)
    lz1 = mm(lb1, w_ref[1])
    lap2 = lap1 + s1 * lz1 - 2.0 * a1 * s1 * sq1
    glz1 = (s1 * gl2).astype(BF16)
    glz0 = (s0 * gl1).astype(BF16)
    gs1 = gl2 * lz1 - cr * whole(x1_ref)
    gz1 = (-2.0 * a1 * gs1 + (6.0 * a1 * a1 - 2.0) * gl2 * sq1) * s1
    gz1b = gz1.astype(BF16)
    gw_ref[1] += outer(h1_ref[...], gz1b) + outer(lb1, glz1)
    gh1 = mm(gz1b, wt_ref[...])
    gs0 = gl1 * (share * lz0) + whole(x0_ref)
    gz0 = (-2.0 * a0 * gs0 + (6.0 * a0 * a0 - 2.0) * gl1 * sq0 + gh1) * s0
    gw_ref[0] += outer(hid_ref[...].astype(BF16), gz0.astype(BF16)) + share * outer(lb0, glz0)
    lapsum = jnp.sum(lap2.reshape(walkers, ne, width), axis=1)
    small = []
    for gz in (gz0, gz1):
        for s in range(2):
            small.append(jnp.sum(jnp.where(spin == s, gz, 0.0), axis=0, keepdims=True))
    gread = jnp.zeros((1, width), F32)
    energy = []
    for i in range(walkers):
        gread -= coeff(i) * (0.5 * lapsum[i:i + 1] + acc_ref[i, 1:2, :])
        energy.append(-0.5 * (jnp.sum(lapsum[i:i + 1] * read, axis=1, keepdims=True) + acc_ref[i, 0:1, 0:1]))
    lane = lax.broadcasted_iota(jnp.int32, (1, LANES), 1)
    here = HALF + walkers * x_index()
    slots = jnp.zeros((1, LANES), F32)
    for i in range(walkers):
        slots = jnp.where(lane == here + i, energy[i], slots)
    extras = [small_part(small + [gread], q, slots, lane) for q in range(NX)]
    block = width // GROUP
    own = core_index()
    for ref, core, sign in ((mine_ref, own, -1.0), (theirs_ref, 1 - own, 1.0)):
        for n, (y, q) in enumerate(YX_ORDER):
            at = pl.multiple_of((y * NC + core) * block, block)
            l, sub = divmod(q, 2)
            rows_q = sign * gw_ref[l, pl.ds(at + 8 * sub, 8), :]
            base = PIECE * n
            ref[base:base + 8, :] = rows_q[:, :LANES]
            ref[base + 8:base + 16, :] = rows_q[:, LANES:]
            ref[base + 16:base + PIECE, :] = sign * extras[q]


def small_part(small, q, slots, lane):
    half, sub = divmod(q, 2)

    def low(r):
        v = small[r][:, half * LANES:(half + 1) * LANES]
        return pltpu.roll(v, HALF, 1) if sub else v

    def high(r):
        v = small[r][:, half * LANES:(half + 1) * LANES]
        return v if sub else pltpu.roll(v, HALF, 1)

    first = lane < HALF
    return jnp.concatenate([jnp.where(first, low(0), high(1)), jnp.where(first, low(2), high(3)),
                            jnp.where(first, low(4), slots)], axis=0)


def x_index():
    return lax.axis_index("x")


def core_index():
    return lax.axis_index("core")


def local_part(hidden0, tangent0, laplace0, spins, weights, spin_bias, readout, cot):
    walkers, tangents, ne, width = tangent0.shape
    rows = walkers * ne
    half = (NY * NX * PIECE, LANES)
    body = functools.partial(local_kernel, walkers=walkers, tangents=tangents, ne=ne, width=width,
                             walkers_all=walkers * NX * NZ)
    full = lambda *shape: pl.BlockSpec(shape, lambda w: (0,) * len(shape))
    wide = pltpu.VMEM((rows, width), F32)
    twice = pltpu.VMEM((walkers, 2 * ne, width), BF16)
    sums = pltpu.VMEM((walkers, ne, width), F32)
    return pl.pallas_call(
        body,
        grid=(1,),
        out_shape=[jax.ShapeDtypeStruct(half, F32)] * 2,
        in_specs=[
            pl.BlockSpec(memory_space=pltpu.SMEM),
            full(walkers * tangents * ne, width),
            full(rows, width),
            full(rows, width),
            full(walkers, ne),
            full(2, width, width),
            full(2, 2, width),
            full(1, width),
        ],
        out_specs=[full(*half)] * 2,
        scratch_shapes=[pltpu.VMEM((width, width), BF16)] + [wide] * 3 + [pltpu.VMEM((rows, width), BF16)]
        + [twice] * 5 + [sums] * 4 + [pltpu.VMEM((2, width, width), F32), pltpu.VMEM((walkers, 2, width), F32)],
        compiler_params=pltpu.CompilerParams(vmem_limit_bytes=VLIM * 1024 * 1024),
        name="local_part",
    )(cot, tangent0.reshape(-1, width), hidden0.reshape(rows, width), laplace0.reshape(rows, width),
      spins, weights, spin_bias, readout.reshape(1, width))


def last_sum_kernel(parts_ref, own_ref, energy_ref, weights_ref, bias_ref, read_ref):
    walkers = energy_ref.shape[0]
    totals = []
    for q in range(NX):
        pieces = [parts_ref[PIECE * n:PIECE * (n + 1), :] for n, (x, _) in enumerate(XZ_ORDER) if x == q]
        total = sum(pieces[1:], pieces[0])
        l, sub = divmod(q, 2)
        weights_ref[l, 8 * sub:8 * sub + 8, :LANES] = total[:8]
        weights_ref[l, 8 * sub:8 * sub + 8, LANES:] = total[8:16]
        totals.append(total[16:])
    lane = lax.broadcasted_iota(jnp.int32, (1, LANES), 1)
    first = lane < HALF

    def small_row(r):
        at = slice(r // 2, r // 2 + 1)
        halves = []
        for half in range(2):
            a, b = totals[2 * half][at], totals[2 * half + 1][at]
            if r % 2 == 0:
                b = pltpu.roll(b, HALF, 1)
            else:
                a = pltpu.roll(a, HALF, 1)
            halves.append(jnp.where(first, a, b))
        return jnp.concatenate(halves, axis=1)

    for l in range(2):
        bias_ref[l] = jnp.concatenate([small_row(2 * l), small_row(2 * l + 1)], axis=0)
    read_ref[...] = small_row(4)[0]
    slots = own_ref[PIECE - 1:PIECE, :]
    here = HALF + walkers * x_index()
    spread = jnp.zeros((1, LANES), F32)
    for i in range(walkers):
        one = jnp.sum(jnp.where(lane == here + i, slots, 0.0), axis=1, keepdims=True)
        spread = jnp.where(lane == i, one, spread)
    energy_ref[...] = spread[0, :walkers]


def last_sum(parts, own, walkers, width):
    shapes = ((walkers,), (2, width // GROUP, width), (2, 2, width), (width,))
    return pl.pallas_call(
        last_sum_kernel,
        out_shape=[jax.ShapeDtypeStruct(s, F32) for s in shapes],
        name="last_sum",
    )(parts.reshape(-1, LANES), own.reshape(PIECE, LANES))


def exchange(pieces, axes, order):
    return lax.all_to_all(pieces, axes, 0, 0, axis_index_groups=[order])


def per_device(hidden0, tangent0, laplace0, spins, weights, spin_bias, readout, energy_cotangent):
    walkers = hidden0.shape[0]
    width = weights.shape[1]
    minus, theirs = local_part(hidden0, tangent0, laplace0, spins, weights, spin_bias, readout, energy_cotangent)
    got = lax.ppermute(theirs, "core", [(0, 1), (1, 0)])
    part = (lax.optimization_barrier(-minus) + got).reshape(NY * NX, PIECE, 1, LANES)
    own = jnp.sum(exchange(part, ("y", "x"), [y * NX + x for y, x in YX_ORDER]), axis=0)
    part = jnp.broadcast_to(own[None], (NX * NZ,) + own.shape)
    return last_sum(exchange(part, ("x", "z"), [x * NZ + z for x, z in XZ_ORDER]), own, walkers, width)


def solution(mesh):
    split = Mesh(mesh.devices.reshape(NX, NZ, NY, NC), ("x", "z", "y", "core"))
    walker, tangent = ("x", "z"), ("y", "core")
    in_specs = (
        P(walker, None, None),
        P(walker, tangent, None, None),
        P(walker, None, None),
        P(walker, None),
        P(),
        P(),
        P(),
        P(walker),
    )
    out_specs = (P(walker), P(None, tangent, None), P(), P())
    return jax.shard_map(
        per_device, mesh=split, in_specs=in_specs, out_specs=out_specs, check_vma=False
    )
```

```python
import functools

import jax
import jax.numpy as jnp
from jax import lax
from jax.experimental import pallas as pl
from jax.experimental.pallas import tpu as pltpu
from jax.sharding import Mesh, PartitionSpec as P

SUBS, SKEW, FINE, VLIM = 4, 1, 1, 60
NX, NZ, NY, NC = 4, 8, 8, 2
GROUP = NY * NC
LANES, HALF = 128, 64
PIECE = 19
STRIDE = 3
X_ORDER = (0, 2, 1, 3)
YX_ORDER = [(STRIDE * k % NY, x) for x in X_ORDER for k in range(NY)]
XZ_ORDER = [(x, STRIDE * k % NZ) for x in X_ORDER for k in range(NZ)]
F32 = jnp.float32
BF16 = jnp.bfloat16


def mm(a, b):
    return lax.dot_general(a, b, (((1,), (0,)), ((), ())), preferred_element_type=F32)


def outer(a, b):
    return lax.dot_general(a, b, (((0,), (0,)), ((), ())), preferred_element_type=F32)


def local_kernel(cot_ref, tan_ref, hid_ref, lap_ref, spin_ref, w_ref, bias_ref, read_ref, mine_ref, theirs_ref,
                 wt_ref, a0_ref, a1_ref, gl1_ref, h1_ref, s0_ref, s1_ref, amp1_ref, b1_ref, b0_ref,
                 sq0_ref, sq1_ref, x0_ref, x1_ref, gw_ref, acc_ref, *, walkers, tangents, ne, width, walkers_all):
    two = 2 * ne
    lo = ne // 16 * 16
    read = read_ref[...]

    def coeff(i):
        return cot_ref[i] * (1.0 / walkers_all)

    def spin_column():
        turned = spin_ref[...].astype(F32).T
        return jnp.concatenate([turned[:, i:i + 1] for i in range(walkers)], axis=0)

    def coeff_rows():
        return jnp.concatenate([jnp.broadcast_to(coeff(i) * read, (ne, width)) for i in range(walkers)], axis=0)

    wt_ref[...] = w_ref[1].T
    spin = spin_column()
    hid0 = hid_ref[...]

    def layer(hid, l):
        bias = jnp.where(spin == 0, bias_ref[l, 0:1, :], bias_ref[l, 1:2, :])
        return jnp.tanh(mm(hid.astype(BF16), w_ref[l]) + bias)

    def keep_twice(ref, v):
        for i in range(walkers):
            one = v[i * ne:(i + 1) * ne]
            ref[i] = jnp.concatenate([one, one], axis=0).astype(BF16)

    a0 = layer(hid0, 0)
    h1 = hid0 + a0
    a1 = layer(h1, 1)
    a0_ref[...] = a0
    a1_ref[...] = a1
    h1_ref[...] = h1.astype(BF16)
    s0 = 1.0 - a0 * a0
    s1 = 1.0 - a1 * a1
    cr = coeff_rows()
    gl2 = -0.5 * cr
    gl1 = gl2 + mm((s1 * gl2).astype(BF16), wt_ref[...])
    gl1_ref[...] = gl1
    keep_twice(s0_ref, s0)
    keep_twice(s1_ref, s1)
    keep_twice(amp1_ref, -cr * s1)
    keep_twice(b1_ref, 2.0 * cr * a1 * s1)
    keep_twice(b0_ref, -4.0 * a0 * s0 * gl1)
    gw_ref[...] = jnp.zeros_like(gw_ref)

    tangents_u = tangents // SUBS
    pairs = tangents_u // 2
    span = tangents_u * ne
    units = [(w, p) for w in range(walkers) for p in range(SUBS)]

    def split(v):
        return v.reshape(pairs, two, width)

    def flat(v):
        return v.reshape(pairs * two, width)

    def fold(v):
        half = v[:pairs // 2] + v[pairs // 2:]
        total = jnp.sum(half.astype(F32), axis=0)
        return total[:ne] + total[ne:]

    def rows_of(p, v):
        a = jnp.broadcast_to(v[2 * p:2 * p + 1], (lo, width)).astype(BF16)
        b = jnp.broadcast_to(v[2 * p + 1:2 * p + 2], (two - lo - 16, width)).astype(BF16)
        mid = jnp.concatenate([jnp.broadcast_to(v[2 * p:2 * p + 1], (ne - lo, width)),
                               jnp.broadcast_to(v[2 * p + 1:2 * p + 2], (16 - ne + lo, width))], axis=0)
        return jnp.concatenate([a, mid.astype(BF16), b], axis=0)

    def add(u, ref, v):
        w, p = units[u]
        ref[w] = v if p == 0 else ref[w] + v

    def tan0_of(u):
        return tan_ref[u * span:(u + 1) * span, :]

    n = len(units)
    z0, tan1, z1, gb, gz1, back, gz0 = ([None] * n for _ in range(7))

    def start(u):
        z0[u] = split(mm(tan0_of(u), w_ref[0]).astype(BF16))

    def first(u):
        w = units[u][0]
        add(u, sq0_ref, fold(z0[u] * z0[u]))
        tan1[u] = split(tan0_of(u)) + s0_ref[w][None] * z0[u]

    def second(u):
        z1[u] = split(mm(flat(tan1[u]), w_ref[1]).astype(BF16))

    def third(u):
        w = units[u][0]
        add(u, sq1_ref, fold(z1[u] * z1[u]))
        tan2 = tan1[u] + s1_ref[w][None] * z1[u]
        cols = jnp.sum(flat(tan2).astype(F32).reshape(tangents_u, ne, width), axis=1)
        g = jnp.sum(cols * read, axis=1, keepdims=True)
        squares = jnp.broadcast_to(jnp.sum(g * g, axis=0, keepdims=True), (1, width))
        add(u, acc_ref, jnp.concatenate([squares, jnp.sum(g * cols, axis=0, keepdims=True)], axis=0))
        gb[u] = jnp.broadcast_to(g, (tangents_u, width))

    def fourth(u):
        w = units[u][0]
        gains = jnp.stack([rows_of(p, gb[u]) for p in range(pairs)])
        add(u, x1_ref, fold(gains * z1[u]))
        gz1[u] = flat(gains * amp1_ref[w][None] + b1_ref[w][None] * z1[u])

    def fifth(u):
        back[u] = split(mm(gz1[u], wt_ref[...]).astype(BF16))

    def outer1(u):
        gw_ref[1] += outer(flat(tan1[u]), gz1[u])

    def sixth(u):
        w = units[u][0]
        pull = gb[u] * (-coeff(w) * read)
        gt1 = back[u] + jnp.stack([rows_of(p, pull) for p in range(pairs)])
        add(u, x0_ref, fold(gt1 * z0[u]))
        gz0[u] = flat(s0_ref[w][None] * gt1 + b0_ref[w][None] * z0[u])

    def outer0(u):
        gw_ref[0] += outer(tan0_of(u), gz0[u])

    stages = [(start,), (first, second), (third, fourth, fifth), (outer1, sixth), (outer0,)]
    if FINE:
        stages = [(start,), (first,), (second,), (third,), (fourth,), (fifth, outer1), (sixth,), (outer0,)]
    if SKEW:
        for tick in range(n + len(stages) - 1):
            for k in reversed(range(len(stages))):
                if 0 <= tick - k < n:
                    for f in stages[k]:
                        f(tick - k)
    else:
        for stage in stages:
            for u in range(n):
                for f in stage:
                    f(u)

    share = 1.0 / GROUP
    spin = spin_column()
    cr = coeff_rows()
    gl2 = -0.5 * cr
    a0, a1, gl1 = a0_ref[...], a1_ref[...], gl1_ref[...]
    s0 = 1.0 - a0 * a0
    s1 = 1.0 - a1 * a1
    whole = lambda ref: ref[...].reshape(walkers * ne, width)
    sq0, sq1 = whole(sq0_ref), whole(sq1_ref)
    lap0 = lap_ref[...]
    lb0 = lap0.astype(BF16)
    lz0 = mm(lb0, w_ref[0])
    lap1 = share * (lap0 + s0 * lz0) - 2.0 * a0 * s0 * sq0
    lb1 = lap1.astype(BF16)
    lz1 = mm(lb1, w_ref[1])
    lap2 = lap1 + s1 * lz1 - 2.0 * a1 * s1 * sq1
    glz1 = (s1 * gl2).astype(BF16)
    glz0 = (s0 * gl1).astype(BF16)
    gs1 = gl2 * lz1 - cr * whole(x1_ref)
    gz1 = (-2.0 * a1 * gs1 + (6.0 * a1 * a1 - 2.0) * gl2 * sq1) * s1
    gz1b = gz1.astype(BF16)
    gw_ref[1] += outer(h1_ref[...], gz1b) + outer(lb1, glz1)
    gh1 = mm(gz1b, wt_ref[...])
    gs0 = gl1 * (share * lz0) + whole(x0_ref)
    gz0 = (-2.0 * a0 * gs0 + (6.0 * a0 * a0 - 2.0) * gl1 * sq0 + gh1) * s0
    gw_ref[0] += outer(hid_ref[...].astype(BF16), gz0.astype(BF16)) + share * outer(lb0, glz0)
    lapsum = jnp.sum(lap2.reshape(walkers, ne, width), axis=1)
    small = []
    for gz in (gz0, gz1):
        for s in range(2):
            small.append(jnp.sum(jnp.where(spin == s, gz, 0.0), axis=0, keepdims=True))
    gread = jnp.zeros((1, width), F32)
    energy = []
    for i in range(walkers):
        gread -= coeff(i) * (0.5 * lapsum[i:i + 1] + acc_ref[i, 1:2, :])
        energy.append(-0.5 * (jnp.sum(lapsum[i:i + 1] * read, axis=1, keepdims=True) + acc_ref[i, 0:1, 0:1]))
    lane = lax.broadcasted_iota(jnp.int32, (1, LANES), 1)
    here = HALF + walkers * x_index()
    slots = jnp.zeros((1, LANES), F32)
    for i in range(walkers):
        slots = jnp.where(lane == here + i, energy[i], slots)
    extras = [small_part(small + [gread], q, slots, lane) for q in range(NX)]
    block = width // GROUP
    own = core_index()
    for ref, core, sign in ((mine_ref, own, -1.0), (theirs_ref, 1 - own, 1.0)):
        for n, (y, q) in enumerate(YX_ORDER):
            at = pl.multiple_of((y * NC + core) * block, block)
            l, sub = divmod(q, 2)
            rows_q = sign * gw_ref[l, pl.ds(at + 8 * sub, 8), :]
            base = PIECE * n
            ref[base:base + 8, :] = rows_q[:, :LANES]
            ref[base + 8:base + 16, :] = rows_q[:, LANES:]
            ref[base + 16:base + PIECE, :] = sign * extras[q]


def small_part(small, q, slots, lane):
    half, sub = divmod(q, 2)

    def low(r):
        v = small[r][:, half * LANES:(half + 1) * LANES]
        return pltpu.roll(v, HALF, 1) if sub else v

    def high(r):
        v = small[r][:, half * LANES:(half + 1) * LANES]
        return v if sub else pltpu.roll(v, HALF, 1)

    first = lane < HALF
    return jnp.concatenate([jnp.where(first, low(0), high(1)), jnp.where(first, low(2), high(3)),
                            jnp.where(first, low(4), slots)], axis=0)


def x_index():
    return lax.axis_index("x")


def core_index():
    return lax.axis_index("core")


def local_part(hidden0, tangent0, laplace0, spins, weights, spin_bias, readout, cot):
    walkers, tangents, ne, width = tangent0.shape
    rows = walkers * ne
    half = (NY * NX * PIECE, LANES)
    body = functools.partial(local_kernel, walkers=walkers, tangents=tangents, ne=ne, width=width,
                             walkers_all=walkers * NX * NZ)
    full = lambda *shape: pl.BlockSpec(shape, lambda w: (0,) * len(shape))
    wide = pltpu.VMEM((rows, width), F32)
    twice = pltpu.VMEM((walkers, 2 * ne, width), BF16)
    sums = pltpu.VMEM((walkers, ne, width), F32)
    return pl.pallas_call(
        body,
        grid=(1,),
        out_shape=[jax.ShapeDtypeStruct(half, F32)] * 2,
        in_specs=[
            pl.BlockSpec(memory_space=pltpu.SMEM),
            full(walkers * tangents * ne, width),
            full(rows, width),
            full(rows, width),
            full(walkers, ne),
            full(2, width, width),
            full(2, 2, width),
            full(1, width),
        ],
        out_specs=[full(*half)] * 2,
        scratch_shapes=[pltpu.VMEM((width, width), BF16)] + [wide] * 3 + [pltpu.VMEM((rows, width), BF16)]
        + [twice] * 5 + [sums] * 4 + [pltpu.VMEM((2, width, width), F32), pltpu.VMEM((walkers, 2, width), F32)],
        compiler_params=pltpu.CompilerParams(vmem_limit_bytes=VLIM * 1024 * 1024),
        name="local_part",
    )(cot, tangent0.reshape(-1, width), hidden0.reshape(rows, width), laplace0.reshape(rows, width),
      spins, weights, spin_bias, readout.reshape(1, width))


def last_sum_kernel(parts_ref, own_ref, energy_ref, weights_ref, bias_ref, read_ref):
    walkers = energy_ref.shape[0]
    totals = []
    for q in range(NX):
        pieces = [parts_ref[PIECE * n:PIECE * (n + 1), :] for n, (x, _) in enumerate(XZ_ORDER) if x == q]
        total = sum(pieces[1:], pieces[0])
        l, sub = divmod(q, 2)
        weights_ref[l, 8 * sub:8 * sub + 8, :LANES] = total[:8]
        weights_ref[l, 8 * sub:8 * sub + 8, LANES:] = total[8:16]
        totals.append(total[16:])
    lane = lax.broadcasted_iota(jnp.int32, (1, LANES), 1)
    first = lane < HALF

    def small_row(r):
        at = slice(r // 2, r // 2 + 1)
        halves = []
        for half in range(2):
            a, b = totals[2 * half][at], totals[2 * half + 1][at]
            if r % 2 == 0:
                b = pltpu.roll(b, HALF, 1)
            else:
                a = pltpu.roll(a, HALF, 1)
            halves.append(jnp.where(first, a, b))
        return jnp.concatenate(halves, axis=1)

    for l in range(2):
        bias_ref[l] = jnp.concatenate([small_row(2 * l), small_row(2 * l + 1)], axis=0)
    read_ref[...] = small_row(4)[0]
    slots = own_ref[PIECE - 1:PIECE, :]
    here = HALF + walkers * x_index()
    spread = jnp.zeros((1, LANES), F32)
    for i in range(walkers):
        one = jnp.sum(jnp.where(lane == here + i, slots, 0.0), axis=1, keepdims=True)
        spread = jnp.where(lane == i, one, spread)
    energy_ref[...] = spread[0, :walkers]


def last_sum(parts, own, walkers, width):
    shapes = ((walkers,), (2, width // GROUP, width), (2, 2, width), (width,))
    return pl.pallas_call(
        last_sum_kernel,
        out_shape=[jax.ShapeDtypeStruct(s, F32) for s in shapes],
        compiler_params=pltpu.CompilerParams(vmem_limit_bytes=4 * 1024 * 1024),
        name="last_sum",
    )(parts.reshape(-1, LANES), own.reshape(PIECE, LANES))


def exchange(pieces, axes, order):
    return lax.all_to_all(pieces, axes, 0, 0, axis_index_groups=[order])


def per_device(hidden0, tangent0, laplace0, spins, weights, spin_bias, readout, energy_cotangent):
    walkers = hidden0.shape[0]
    width = weights.shape[1]
    minus, theirs = local_part(hidden0, tangent0, laplace0, spins, weights, spin_bias, readout, energy_cotangent)
    got = lax.ppermute(theirs, "core", [(0, 1), (1, 0)])
    part = (lax.optimization_barrier(-minus) + got).reshape(NY * NX, PIECE, 1, LANES)
    own = jnp.sum(exchange(part, ("y", "x"), [y * NX + x for y, x in YX_ORDER]), axis=0)
    part = jnp.broadcast_to(own[None], (NX * NZ,) + own.shape)
    return last_sum(exchange(part, ("x", "z"), [x * NZ + z for x, z in XZ_ORDER]), own, walkers, width)


def solution(mesh):
    split = Mesh(mesh.devices.reshape(NX, NZ, NY, NC), ("x", "z", "y", "core"))
    walker, tangent = ("x", "z"), ("y", "core")
    in_specs = (
        P(walker, None, None),
        P(walker, tangent, None, None),
        P(walker, None, None),
        P(walker, None),
        P(),
        P(),
        P(),
        P(walker),
    )
    out_specs = (P(walker), P(None, tangent, None), P(), P())
    return jax.shard_map(
        per_device, mesh=split, in_specs=in_specs, out_specs=out_specs, check_vma=False
    )
```

```python
import functools

import jax
import jax.numpy as jnp
from jax import lax
from jax.experimental import pallas as pl
from jax.experimental.pallas import tpu as pltpu
from jax.sharding import Mesh, PartitionSpec as P

SUBS = 4
NX, NZ, NY, NC = 4, 8, 8, 2
GROUP = NY * NC
LANES, HALF = 128, 64
PIECE = 19
F32 = jnp.float32
BF16 = jnp.bfloat16


def mm(a, b):
    return lax.dot_general(a, b, (((1,), (0,)), ((), ())), preferred_element_type=F32)


def outer(a, b):
    return lax.dot_general(a, b, (((0,), (0,)), ((), ())), preferred_element_type=F32)


def local_kernel(cot_ref, tan_ref, hid_ref, lap_ref, spin_ref, w_ref, bias_ref, read_ref, mine_ref, theirs_ref,
                 wt_ref, a0_ref, a1_ref, gl1_ref, h1_ref, s0_ref, s1_ref, amp1_ref, b1_ref, b0_ref,
                 sq0_ref, sq1_ref, x0_ref, x1_ref, gw_ref, acc_ref, *, walkers, tangents, ne, width, walkers_all):
    two = 2 * ne
    lo = ne // 16 * 16
    read = read_ref[...]

    def coeff(i):
        return cot_ref[i] * (1.0 / walkers_all)

    def spin_column():
        turned = spin_ref[...].astype(F32).T
        return jnp.concatenate([turned[:, i:i + 1] for i in range(walkers)], axis=0)

    def coeff_rows():
        return jnp.concatenate([jnp.broadcast_to(coeff(i) * read, (ne, width)) for i in range(walkers)], axis=0)

    wt_ref[...] = w_ref[1].T
    spin = spin_column()
    hid0 = hid_ref[...]

    def layer(hid, l):
        bias = jnp.where(spin == 0, bias_ref[l, 0:1, :], bias_ref[l, 1:2, :])
        return jnp.tanh(mm(hid.astype(BF16), w_ref[l]) + bias)

    def keep_twice(ref, v):
        for i in range(walkers):
            one = v[i * ne:(i + 1) * ne]
            ref[i] = jnp.concatenate([one, one], axis=0).astype(BF16)

    a0 = layer(hid0, 0)
    h1 = hid0 + a0
    a1 = layer(h1, 1)
    a0_ref[...] = a0
    a1_ref[...] = a1
    h1_ref[...] = h1.astype(BF16)
    s0 = 1.0 - a0 * a0
    s1 = 1.0 - a1 * a1
    cr = coeff_rows()
    gl2 = -0.5 * cr
    gl1 = gl2 + mm((s1 * gl2).astype(BF16), wt_ref[...])
    gl1_ref[...] = gl1
    keep_twice(s0_ref, s0)
    keep_twice(s1_ref, s1)
    keep_twice(amp1_ref, -cr * s1)
    keep_twice(b1_ref, 2.0 * cr * a1 * s1)
    keep_twice(b0_ref, -4.0 * a0 * s0 * gl1)
    gw_ref[...] = jnp.zeros_like(gw_ref)

    tangents_u = tangents // SUBS
    pairs = tangents_u // 2
    span = tangents_u * ne
    units = [(w, p) for w in range(walkers) for p in range(SUBS)]

    def split(v):
        return v.reshape(pairs, two, width)

    def flat(v):
        return v.reshape(pairs * two, width)

    def fold(v):
        half = v[:pairs // 2] + v[pairs // 2:]
        total = jnp.sum(half.astype(F32), axis=0)
        return total[:ne] + total[ne:]

    def rows_of(p, v):
        a = jnp.broadcast_to(v[2 * p:2 * p + 1], (lo, width)).astype(BF16)
        b = jnp.broadcast_to(v[2 * p + 1:2 * p + 2], (two - lo - 16, width)).astype(BF16)
        mid = jnp.concatenate([jnp.broadcast_to(v[2 * p:2 * p + 1], (ne - lo, width)),
                               jnp.broadcast_to(v[2 * p + 1:2 * p + 2], (16 - ne + lo, width))], axis=0)
        return jnp.concatenate([a, mid.astype(BF16), b], axis=0)

    def add(u, ref, v):
        w, p = units[u]
        ref[w] = v if p == 0 else ref[w] + v

    def tan0_of(u):
        return tan_ref[u * span:(u + 1) * span, :]

    n = len(units)
    z0, tan1, z1, gb, gz1, back, gz0 = ([None] * n for _ in range(7))

    def start(u):
        z0[u] = split(mm(tan0_of(u), w_ref[0]).astype(BF16))

    def first(u):
        w = units[u][0]
        add(u, sq0_ref, fold(z0[u] * z0[u]))
        tan1[u] = split(tan0_of(u)) + s0_ref[w][None] * z0[u]

    def second(u):
        z1[u] = split(mm(flat(tan1[u]), w_ref[1]).astype(BF16))

    def third(u):
        w = units[u][0]
        add(u, sq1_ref, fold(z1[u] * z1[u]))
        tan2 = tan1[u] + s1_ref[w][None] * z1[u]
        cols = jnp.sum(flat(tan2).astype(F32).reshape(tangents_u, ne, width), axis=1)
        g = jnp.sum(cols * read, axis=1, keepdims=True)
        squares = jnp.broadcast_to(jnp.sum(g * g, axis=0, keepdims=True), (1, width))
        add(u, acc_ref, jnp.concatenate([squares, jnp.sum(g * cols, axis=0, keepdims=True)], axis=0))
        gb[u] = jnp.broadcast_to(g, (tangents_u, width))

    def fourth(u):
        w = units[u][0]
        gains = jnp.stack([rows_of(p, gb[u]) for p in range(pairs)])
        add(u, x1_ref, fold(gains * z1[u]))
        gz1[u] = flat(gains * amp1_ref[w][None] + b1_ref[w][None] * z1[u])

    def fifth(u):
        back[u] = split(mm(gz1[u], wt_ref[...]).astype(BF16))

    def outer1(u):
        gw_ref[1] += outer(flat(tan1[u]), gz1[u])

    def sixth(u):
        w = units[u][0]
        pull = gb[u] * (-coeff(w) * read)
        gt1 = back[u] + jnp.stack([rows_of(p, pull) for p in range(pairs)])
        add(u, x0_ref, fold(gt1 * z0[u]))
        gz0[u] = flat(s0_ref[w][None] * gt1 + b0_ref[w][None] * z0[u])

    def outer0(u):
        gw_ref[0] += outer(tan0_of(u), gz0[u])

    stages = [(start,), (first,), (second,), (third,), (fourth,), (fifth, outer1), (sixth,), (outer0,)]
    for tick in range(n + len(stages) - 1):
        for k in reversed(range(len(stages))):
            if 0 <= tick - k < n:
                for f in stages[k]:
                    f(tick - k)

    share = 1.0 / GROUP
    spin = spin_column()
    cr = coeff_rows()
    gl2 = -0.5 * cr
    a0, a1, gl1 = a0_ref[...], a1_ref[...], gl1_ref[...]
    s0 = 1.0 - a0 * a0
    s1 = 1.0 - a1 * a1
    whole = lambda ref: ref[...].reshape(walkers * ne, width)
    sq0, sq1 = whole(sq0_ref), whole(sq1_ref)
    lap0 = lap_ref[...]
    lb0 = lap0.astype(BF16)
    lz0 = mm(lb0, w_ref[0])
    lap1 = share * (lap0 + s0 * lz0) - 2.0 * a0 * s0 * sq0
    lb1 = lap1.astype(BF16)
    lz1 = mm(lb1, w_ref[1])
    lap2 = lap1 + s1 * lz1 - 2.0 * a1 * s1 * sq1
    glz1 = (s1 * gl2).astype(BF16)
    glz0 = (s0 * gl1).astype(BF16)
    gs1 = gl2 * lz1 - cr * whole(x1_ref)
    gz1 = (-2.0 * a1 * gs1 + (6.0 * a1 * a1 - 2.0) * gl2 * sq1) * s1
    gz1b = gz1.astype(BF16)
    gw_ref[1] += outer(h1_ref[...], gz1b) + outer(lb1, glz1)
    gh1 = mm(gz1b, wt_ref[...])
    gs0 = gl1 * (share * lz0) + whole(x0_ref)
    gz0 = (-2.0 * a0 * gs0 + (6.0 * a0 * a0 - 2.0) * gl1 * sq0 + gh1) * s0
    gw_ref[0] += outer(hid_ref[...].astype(BF16), gz0.astype(BF16)) + share * outer(lb0, glz0)
    lapsum = jnp.sum(lap2.reshape(walkers, ne, width), axis=1)
    small = []
    for gz in (gz0, gz1):
        for s in range(2):
            small.append(jnp.sum(jnp.where(spin == s, gz, 0.0), axis=0, keepdims=True))
    gread = jnp.zeros((1, width), F32)
    energy = []
    for i in range(walkers):
        gread -= coeff(i) * (0.5 * lapsum[i:i + 1] + acc_ref[i, 1:2, :])
        energy.append(-0.5 * (jnp.sum(lapsum[i:i + 1] * read, axis=1, keepdims=True) + acc_ref[i, 0:1, 0:1]))
    lane = lax.broadcasted_iota(jnp.int32, (1, LANES), 1)
    here = HALF + walkers * x_index()
    slots = jnp.zeros((1, LANES), F32)
    for i in range(walkers):
        slots = jnp.where(lane == here + i, energy[i], slots)
    extras = [small_part(small + [gread], q, slots, lane) for q in range(NX)]
    block = width // GROUP
    own = core_index()
    for ref, core, sign in ((mine_ref, own, -1.0), (theirs_ref, 1 - own, 1.0)):
        for y in range(NY):
            at = pl.multiple_of((y * NC + core) * block, block)
            for q in range(NX):
                l, sub = divmod(q, 2)
                rows_q = sign * gw_ref[l, pl.ds(at + 8 * sub, 8), :]
                base = PIECE * (y * NX + q)
                ref[base:base + 8, :] = rows_q[:, :LANES]
                ref[base + 8:base + 16, :] = rows_q[:, LANES:]
                ref[base + 16:base + PIECE, :] = sign * extras[q]


def small_part(small, q, slots, lane):
    half, sub = divmod(q, 2)

    def low(r):
        v = small[r][:, half * LANES:(half + 1) * LANES]
        return pltpu.roll(v, HALF, 1) if sub else v

    def high(r):
        v = small[r][:, half * LANES:(half + 1) * LANES]
        return v if sub else pltpu.roll(v, HALF, 1)

    first = lane < HALF
    return jnp.concatenate([jnp.where(first, low(0), high(1)), jnp.where(first, low(2), high(3)),
                            jnp.where(first, low(4), slots)], axis=0)


def x_index():
    return lax.axis_index("x")


def core_index():
    return lax.axis_index("core")


def local_part(hidden0, tangent0, laplace0, spins, weights, spin_bias, readout, cot):
    walkers, tangents, ne, width = tangent0.shape
    rows = walkers * ne
    half = (NY * NX * PIECE, LANES)
    body = functools.partial(local_kernel, walkers=walkers, tangents=tangents, ne=ne, width=width,
                             walkers_all=walkers * NX * NZ)
    full = lambda *shape: pl.BlockSpec(shape, lambda w: (0,) * len(shape))
    wide = pltpu.VMEM((rows, width), F32)
    twice = pltpu.VMEM((walkers, 2 * ne, width), BF16)
    sums = pltpu.VMEM((walkers, ne, width), F32)
    return pl.pallas_call(
        body,
        grid=(1,),
        out_shape=[jax.ShapeDtypeStruct(half, F32)] * 2,
        in_specs=[
            pl.BlockSpec(memory_space=pltpu.SMEM),
            full(walkers * tangents * ne, width),
            full(rows, width),
            full(rows, width),
            full(walkers, ne),
            full(2, width, width),
            full(2, 2, width),
            full(1, width),
        ],
        out_specs=[full(*half)] * 2,
        scratch_shapes=[pltpu.VMEM((width, width), BF16)] + [wide] * 3 + [pltpu.VMEM((rows, width), BF16)]
        + [twice] * 5 + [sums] * 4 + [pltpu.VMEM((2, width, width), F32), pltpu.VMEM((walkers, 2, width), F32)],
        compiler_params=pltpu.CompilerParams(vmem_limit_bytes=60 * 1024 * 1024),
        name="local_part",
    )(cot, tangent0.reshape(-1, width), hidden0.reshape(rows, width), laplace0.reshape(rows, width),
      spins, weights, spin_bias, readout.reshape(1, width))


def last_sum_kernel(parts_ref, own_ref, energy_ref, weights_ref, bias_ref, read_ref):
    walkers = energy_ref.shape[0]
    totals = []
    for q in range(NX):
        pieces = [parts_ref[PIECE * (q * NZ + z):PIECE * (q * NZ + z + 1), :] for z in range(NZ)]
        total = sum(pieces[1:], pieces[0])
        l, sub = divmod(q, 2)
        weights_ref[l, 8 * sub:8 * sub + 8, :LANES] = total[:8]
        weights_ref[l, 8 * sub:8 * sub + 8, LANES:] = total[8:16]
        totals.append(total[16:])
    lane = lax.broadcasted_iota(jnp.int32, (1, LANES), 1)
    first = lane < HALF

    def small_row(r):
        at = slice(r // 2, r // 2 + 1)
        halves = []
        for half in range(2):
            a, b = totals[2 * half][at], totals[2 * half + 1][at]
            if r % 2 == 0:
                b = pltpu.roll(b, HALF, 1)
            else:
                a = pltpu.roll(a, HALF, 1)
            halves.append(jnp.where(first, a, b))
        return jnp.concatenate(halves, axis=1)

    for l in range(2):
        bias_ref[l] = jnp.concatenate([small_row(2 * l), small_row(2 * l + 1)], axis=0)
    read_ref[...] = small_row(4)[0]
    slots = own_ref[PIECE - 1:PIECE, :]
    here = HALF + walkers * x_index()
    spread = jnp.zeros((1, LANES), F32)
    for i in range(walkers):
        one = jnp.sum(jnp.where(lane == here + i, slots, 0.0), axis=1, keepdims=True)
        spread = jnp.where(lane == i, one, spread)
    energy_ref[...] = spread[0, :walkers]


def last_sum(parts, own, walkers, width):
    shapes = ((walkers,), (2, width // GROUP, width), (2, 2, width), (width,))
    return pl.pallas_call(
        last_sum_kernel,
        out_shape=[jax.ShapeDtypeStruct(s, F32) for s in shapes],
        compiler_params=pltpu.CompilerParams(vmem_limit_bytes=4 * 1024 * 1024),
        name="last_sum",
    )(parts.reshape(-1, LANES), own.reshape(PIECE, LANES))


def per_device(hidden0, tangent0, laplace0, spins, weights, spin_bias, readout, energy_cotangent):
    walkers = hidden0.shape[0]
    width = weights.shape[1]
    minus, theirs = local_part(hidden0, tangent0, laplace0, spins, weights, spin_bias, readout, energy_cotangent)
    got = lax.ppermute(theirs, "core", [(0, 1), (1, 0)])
    part = (lax.optimization_barrier(-minus) + got).reshape(NY * NX, PIECE, 1, LANES)
    own = jnp.sum(lax.all_to_all(part, ("y", "x"), 0, 0), axis=0)
    part = jnp.broadcast_to(own[None], (NX * NZ,) + own.shape)
    return last_sum(lax.all_to_all(part, ("x", "z"), 0, 0), own, walkers, width)


def solution(mesh):
    split = Mesh(mesh.devices.reshape(NX, NZ, NY, NC), ("x", "z", "y", "core"))
    walker, tangent = ("x", "z"), ("y", "core")
    in_specs = (
        P(walker, None, None),
        P(walker, tangent, None, None),
        P(walker, None, None),
        P(walker, None),
        P(),
        P(),
        P(),
        P(walker),
    )
    out_specs = (P(walker), P(None, tangent, None), P(), P())
    return jax.shard_map(
        per_device, mesh=split, in_specs=in_specs, out_specs=out_specs, check_vma=False
    )
```

```python
import functools

import jax
import jax.numpy as jnp
from jax import lax
from jax.experimental import pallas as pl
from jax.experimental.pallas import tpu as pltpu
from jax.sharding import Mesh, PartitionSpec as P

SUBS = 4
NX, NZ, NY, NC = 4, 8, 8, 2
GROUP = NY * NC
LANES, HALF = 128, 64
PIECE = 19
YX_ORDER = [(y, x) for y in range(NY) for x in range(NX)][::-1]
XZ_ORDER = [(x, z) for x in range(NX) for z in range(NZ)][::-1]
F32 = jnp.float32
BF16 = jnp.bfloat16


def mm(a, b):
    return lax.dot_general(a, b, (((1,), (0,)), ((), ())), preferred_element_type=F32)


def outer(a, b):
    return lax.dot_general(a, b, (((0,), (0,)), ((), ())), preferred_element_type=F32)


def local_kernel(cot_ref, tan_ref, hid_ref, lap_ref, spin_ref, w_ref, bias_ref, read_ref, mine_ref, theirs_ref,
                 wt_ref, a0_ref, a1_ref, gl1_ref, h1_ref, s0_ref, s1_ref, amp1_ref, b1_ref, b0_ref,
                 sq0_ref, sq1_ref, x0_ref, x1_ref, gw_ref, acc_ref, *, walkers, tangents, ne, width, walkers_all):
    two = 2 * ne
    lo = ne // 16 * 16
    read = read_ref[...]

    def coeff(i):
        return cot_ref[i] * (1.0 / walkers_all)

    def spin_column():
        turned = spin_ref[...].astype(F32).T
        return jnp.concatenate([turned[:, i:i + 1] for i in range(walkers)], axis=0)

    def coeff_rows():
        return jnp.concatenate([jnp.broadcast_to(coeff(i) * read, (ne, width)) for i in range(walkers)], axis=0)

    wt_ref[...] = w_ref[1].T
    spin = spin_column()
    hid0 = hid_ref[...]

    def layer(hid, l):
        bias = jnp.where(spin == 0, bias_ref[l, 0:1, :], bias_ref[l, 1:2, :])
        return jnp.tanh(mm(hid.astype(BF16), w_ref[l]) + bias)

    def keep_twice(ref, v):
        for i in range(walkers):
            one = v[i * ne:(i + 1) * ne]
            ref[i] = jnp.concatenate([one, one], axis=0).astype(BF16)

    a0 = layer(hid0, 0)
    h1 = hid0 + a0
    a1 = layer(h1, 1)
    a0_ref[...] = a0
    a1_ref[...] = a1
    h1_ref[...] = h1.astype(BF16)
    s0 = 1.0 - a0 * a0
    s1 = 1.0 - a1 * a1
    cr = coeff_rows()
    gl2 = -0.5 * cr
    gl1 = gl2 + mm((s1 * gl2).astype(BF16), wt_ref[...])
    gl1_ref[...] = gl1
    keep_twice(s0_ref, s0)
    keep_twice(s1_ref, s1)
    keep_twice(amp1_ref, -cr * s1)
    keep_twice(b1_ref, 2.0 * cr * a1 * s1)
    keep_twice(b0_ref, -4.0 * a0 * s0 * gl1)
    gw_ref[...] = jnp.zeros_like(gw_ref)

    tangents_u = tangents // SUBS
    pairs = tangents_u // 2
    span = tangents_u * ne
    units = [(w, p) for w in range(walkers) for p in range(SUBS)]

    def split(v):
        return v.reshape(pairs, two, width)

    def flat(v):
        return v.reshape(pairs * two, width)

    def fold(v):
        half = v[:pairs // 2] + v[pairs // 2:]
        total = jnp.sum(half.astype(F32), axis=0)
        return total[:ne] + total[ne:]

    def rows_of(p, v):
        a = jnp.broadcast_to(v[2 * p:2 * p + 1], (lo, width)).astype(BF16)
        b = jnp.broadcast_to(v[2 * p + 1:2 * p + 2], (two - lo - 16, width)).astype(BF16)
        mid = jnp.concatenate([jnp.broadcast_to(v[2 * p:2 * p + 1], (ne - lo, width)),
                               jnp.broadcast_to(v[2 * p + 1:2 * p + 2], (16 - ne + lo, width))], axis=0)
        return jnp.concatenate([a, mid.astype(BF16), b], axis=0)

    def add(u, ref, v):
        w, p = units[u]
        ref[w] = v if p == 0 else ref[w] + v

    def tan0_of(u):
        return tan_ref[u * span:(u + 1) * span, :]

    n = len(units)
    z0, tan1, z1, gb, gz1, back, gz0 = ([None] * n for _ in range(7))

    def start(u):
        z0[u] = split(mm(tan0_of(u), w_ref[0]).astype(BF16))

    def first(u):
        w = units[u][0]
        add(u, sq0_ref, fold(z0[u] * z0[u]))
        tan1[u] = split(tan0_of(u)) + s0_ref[w][None] * z0[u]

    def second(u):
        z1[u] = split(mm(flat(tan1[u]), w_ref[1]).astype(BF16))

    def third(u):
        w = units[u][0]
        add(u, sq1_ref, fold(z1[u] * z1[u]))
        tan2 = tan1[u] + s1_ref[w][None] * z1[u]
        cols = jnp.sum(flat(tan2).astype(F32).reshape(tangents_u, ne, width), axis=1)
        g = jnp.sum(cols * read, axis=1, keepdims=True)
        squares = jnp.broadcast_to(jnp.sum(g * g, axis=0, keepdims=True), (1, width))
        add(u, acc_ref, jnp.concatenate([squares, jnp.sum(g * cols, axis=0, keepdims=True)], axis=0))
        gb[u] = jnp.broadcast_to(g, (tangents_u, width))

    def fourth(u):
        w = units[u][0]
        gains = jnp.stack([rows_of(p, gb[u]) for p in range(pairs)])
        add(u, x1_ref, fold(gains * z1[u]))
        gz1[u] = flat(gains * amp1_ref[w][None] + b1_ref[w][None] * z1[u])

    def fifth(u):
        back[u] = split(mm(gz1[u], wt_ref[...]).astype(BF16))

    def outer1(u):
        gw_ref[1] += outer(flat(tan1[u]), gz1[u])

    def sixth(u):
        w = units[u][0]
        pull = gb[u] * (-coeff(w) * read)
        gt1 = back[u] + jnp.stack([rows_of(p, pull) for p in range(pairs)])
        add(u, x0_ref, fold(gt1 * z0[u]))
        gz0[u] = flat(s0_ref[w][None] * gt1 + b0_ref[w][None] * z0[u])

    def outer0(u):
        gw_ref[0] += outer(tan0_of(u), gz0[u])

    stages = [(start,), (first,), (second,), (third,), (fourth,), (fifth, outer1), (sixth,), (outer0,)]
    for tick in range(n + len(stages) - 1):
        for k in reversed(range(len(stages))):
            if 0 <= tick - k < n:
                for f in stages[k]:
                    f(tick - k)

    share = 1.0 / GROUP
    spin = spin_column()
    cr = coeff_rows()
    gl2 = -0.5 * cr
    a0, a1, gl1 = a0_ref[...], a1_ref[...], gl1_ref[...]
    s0 = 1.0 - a0 * a0
    s1 = 1.0 - a1 * a1
    whole = lambda ref: ref[...].reshape(walkers * ne, width)
    sq0, sq1 = whole(sq0_ref), whole(sq1_ref)
    lap0 = lap_ref[...]
    lb0 = lap0.astype(BF16)
    lz0 = mm(lb0, w_ref[0])
    lap1 = share * (lap0 + s0 * lz0) - 2.0 * a0 * s0 * sq0
    lb1 = lap1.astype(BF16)
    lz1 = mm(lb1, w_ref[1])
    lap2 = lap1 + s1 * lz1 - 2.0 * a1 * s1 * sq1
    glz1 = (s1 * gl2).astype(BF16)
    glz0 = (s0 * gl1).astype(BF16)
    gs1 = gl2 * lz1 - cr * whole(x1_ref)
    gz1 = (-2.0 * a1 * gs1 + (6.0 * a1 * a1 - 2.0) * gl2 * sq1) * s1
    gz1b = gz1.astype(BF16)
    gw_ref[1] += outer(h1_ref[...], gz1b) + outer(lb1, glz1)
    gh1 = mm(gz1b, wt_ref[...])
    gs0 = gl1 * (share * lz0) + whole(x0_ref)
    gz0 = (-2.0 * a0 * gs0 + (6.0 * a0 * a0 - 2.0) * gl1 * sq0 + gh1) * s0
    gw_ref[0] += outer(hid_ref[...].astype(BF16), gz0.astype(BF16)) + share * outer(lb0, glz0)
    lapsum = jnp.sum(lap2.reshape(walkers, ne, width), axis=1)
    small = []
    for gz in (gz0, gz1):
        for s in range(2):
            small.append(jnp.sum(jnp.where(spin == s, gz, 0.0), axis=0, keepdims=True))
    gread = jnp.zeros((1, width), F32)
    energy = []
    for i in range(walkers):
        gread -= coeff(i) * (0.5 * lapsum[i:i + 1] + acc_ref[i, 1:2, :])
        energy.append(-0.5 * (jnp.sum(lapsum[i:i + 1] * read, axis=1, keepdims=True) + acc_ref[i, 0:1, 0:1]))
    lane = lax.broadcasted_iota(jnp.int32, (1, LANES), 1)
    here = HALF + walkers * x_index()
    slots = jnp.zeros((1, LANES), F32)
    for i in range(walkers):
        slots = jnp.where(lane == here + i, energy[i], slots)
    extras = [small_part(small + [gread], q, slots, lane) for q in range(NX)]
    block = width // GROUP
    own = core_index()
    for ref, core, sign in ((mine_ref, own, -1.0), (theirs_ref, 1 - own, 1.0)):
        for n, (y, q) in enumerate(YX_ORDER):
            at = pl.multiple_of((y * NC + core) * block, block)
            l, sub = divmod(q, 2)
            rows_q = sign * gw_ref[l, pl.ds(at + 8 * sub, 8), :]
            base = PIECE * n
            ref[base:base + 8, :] = rows_q[:, :LANES]
            ref[base + 8:base + 16, :] = rows_q[:, LANES:]
            ref[base + 16:base + PIECE, :] = sign * extras[q]


def small_part(small, q, slots, lane):
    half, sub = divmod(q, 2)

    def low(r):
        v = small[r][:, half * LANES:(half + 1) * LANES]
        return pltpu.roll(v, HALF, 1) if sub else v

    def high(r):
        v = small[r][:, half * LANES:(half + 1) * LANES]
        return v if sub else pltpu.roll(v, HALF, 1)

    first = lane < HALF
    return jnp.concatenate([jnp.where(first, low(0), high(1)), jnp.where(first, low(2), high(3)),
                            jnp.where(first, low(4), slots)], axis=0)


def x_index():
    return lax.axis_index("x")


def core_index():
    return lax.axis_index("core")


def local_part(hidden0, tangent0, laplace0, spins, weights, spin_bias, readout, cot):
    walkers, tangents, ne, width = tangent0.shape
    rows = walkers * ne
    half = (NY * NX * PIECE, LANES)
    body = functools.partial(local_kernel, walkers=walkers, tangents=tangents, ne=ne, width=width,
                             walkers_all=walkers * NX * NZ)
    full = lambda *shape: pl.BlockSpec(shape, lambda w: (0,) * len(shape))
    wide = pltpu.VMEM((rows, width), F32)
    twice = pltpu.VMEM((walkers, 2 * ne, width), BF16)
    sums = pltpu.VMEM((walkers, ne, width), F32)
    return pl.pallas_call(
        body,
        grid=(1,),
        out_shape=[jax.ShapeDtypeStruct(half, F32)] * 2,
        in_specs=[
            pl.BlockSpec(memory_space=pltpu.SMEM),
            full(walkers * tangents * ne, width),
            full(rows, width),
            full(rows, width),
            full(walkers, ne),
            full(2, width, width),
            full(2, 2, width),
            full(1, width),
        ],
        out_specs=[full(*half)] * 2,
        scratch_shapes=[pltpu.VMEM((width, width), BF16)] + [wide] * 3 + [pltpu.VMEM((rows, width), BF16)]
        + [twice] * 5 + [sums] * 4 + [pltpu.VMEM((2, width, width), F32), pltpu.VMEM((walkers, 2, width), F32)],
        compiler_params=pltpu.CompilerParams(vmem_limit_bytes=60 * 1024 * 1024),
        name="local_part",
    )(cot, tangent0.reshape(-1, width), hidden0.reshape(rows, width), laplace0.reshape(rows, width),
      spins, weights, spin_bias, readout.reshape(1, width))


def last_sum_kernel(parts_ref, own_ref, energy_ref, weights_ref, bias_ref, read_ref):
    walkers = energy_ref.shape[0]
    totals = []
    for q in range(NX):
        pieces = [parts_ref[PIECE * n:PIECE * (n + 1), :] for n, (x, _) in enumerate(XZ_ORDER) if x == q]
        total = sum(pieces[1:], pieces[0])
        l, sub = divmod(q, 2)
        weights_ref[l, 8 * sub:8 * sub + 8, :LANES] = total[:8]
        weights_ref[l, 8 * sub:8 * sub + 8, LANES:] = total[8:16]
        totals.append(total[16:])
    lane = lax.broadcasted_iota(jnp.int32, (1, LANES), 1)
    first = lane < HALF

    def small_row(r):
        at = slice(r // 2, r // 2 + 1)
        halves = []
        for half in range(2):
            a, b = totals[2 * half][at], totals[2 * half + 1][at]
            if r % 2 == 0:
                b = pltpu.roll(b, HALF, 1)
            else:
                a = pltpu.roll(a, HALF, 1)
            halves.append(jnp.where(first, a, b))
        return jnp.concatenate(halves, axis=1)

    for l in range(2):
        bias_ref[l] = jnp.concatenate([small_row(2 * l), small_row(2 * l + 1)], axis=0)
    read_ref[...] = small_row(4)[0]
    slots = own_ref[PIECE - 1:PIECE, :]
    here = HALF + walkers * x_index()
    spread = jnp.zeros((1, LANES), F32)
    for i in range(walkers):
        one = jnp.sum(jnp.where(lane == here + i, slots, 0.0), axis=1, keepdims=True)
        spread = jnp.where(lane == i, one, spread)
    energy_ref[...] = spread[0, :walkers]


def last_sum(parts, own, walkers, width):
    shapes = ((walkers,), (2, width // GROUP, width), (2, 2, width), (width,))
    return pl.pallas_call(
        last_sum_kernel,
        out_shape=[jax.ShapeDtypeStruct(s, F32) for s in shapes],
        compiler_params=pltpu.CompilerParams(vmem_limit_bytes=4 * 1024 * 1024),
        name="last_sum",
    )(parts.reshape(-1, LANES), own.reshape(PIECE, LANES))


def exchange(pieces, axes, order):
    return lax.all_to_all(pieces, axes, 0, 0, axis_index_groups=[order])


def per_device(hidden0, tangent0, laplace0, spins, weights, spin_bias, readout, energy_cotangent):
    walkers = hidden0.shape[0]
    width = weights.shape[1]
    minus, theirs = local_part(hidden0, tangent0, laplace0, spins, weights, spin_bias, readout, energy_cotangent)
    got = lax.ppermute(theirs, "core", [(0, 1), (1, 0)])
    part = (lax.optimization_barrier(-minus) + got).reshape(NY * NX, PIECE, 1, LANES)
    own = jnp.sum(exchange(part, ("y", "x"), [y * NX + x for y, x in YX_ORDER]), axis=0)
    part = jnp.broadcast_to(own[None], (NX * NZ,) + own.shape)
    return last_sum(exchange(part, ("x", "z"), [x * NZ + z for x, z in XZ_ORDER]), own, walkers, width)


def solution(mesh):
    split = Mesh(mesh.devices.reshape(NX, NZ, NY, NC), ("x", "z", "y", "core"))
    walker, tangent = ("x", "z"), ("y", "core")
    in_specs = (
        P(walker, None, None),
        P(walker, tangent, None, None),
        P(walker, None, None),
        P(walker, None),
        P(),
        P(),
        P(),
        P(walker),
    )
    out_specs = (P(walker), P(None, tangent, None), P(), P())
    return jax.shard_map(
        per_device, mesh=split, in_specs=in_specs, out_specs=out_specs, check_vma=False
    )
```

```python
import functools

import jax
import jax.numpy as jnp
from jax import lax
from jax.experimental import pallas as pl
from jax.experimental.pallas import tpu as pltpu
from jax.sharding import Mesh, PartitionSpec as P

SUBS = 4
NX, NZ, NY, NC = 4, 8, 8, 2
GROUP = NY * NC
LANES, HALF = 128, 64
PIECE = 19
YX_ORDER = [(y, x) for x in range(NX) for y in range(NY)][::-1]
XZ_ORDER = [(x, z) for z in range(NZ) for x in range(NX)][::-1]
F32 = jnp.float32
BF16 = jnp.bfloat16


def mm(a, b):
    return lax.dot_general(a, b, (((1,), (0,)), ((), ())), preferred_element_type=F32)


def outer(a, b):
    return lax.dot_general(a, b, (((0,), (0,)), ((), ())), preferred_element_type=F32)


def local_kernel(cot_ref, tan_ref, hid_ref, lap_ref, spin_ref, w_ref, bias_ref, read_ref, mine_ref, theirs_ref,
                 wt_ref, a0_ref, a1_ref, gl1_ref, h1_ref, s0_ref, s1_ref, amp1_ref, b1_ref, b0_ref,
                 sq0_ref, sq1_ref, x0_ref, x1_ref, gw_ref, acc_ref, *, walkers, tangents, ne, width, walkers_all):
    two = 2 * ne
    lo = ne // 16 * 16
    read = read_ref[...]

    def coeff(i):
        return cot_ref[i] * (1.0 / walkers_all)

    def spin_column():
        turned = spin_ref[...].astype(F32).T
        return jnp.concatenate([turned[:, i:i + 1] for i in range(walkers)], axis=0)

    def coeff_rows():
        return jnp.concatenate([jnp.broadcast_to(coeff(i) * read, (ne, width)) for i in range(walkers)], axis=0)

    wt_ref[...] = w_ref[1].T
    spin = spin_column()
    hid0 = hid_ref[...]

    def layer(hid, l):
        bias = jnp.where(spin == 0, bias_ref[l, 0:1, :], bias_ref[l, 1:2, :])
        return jnp.tanh(mm(hid.astype(BF16), w_ref[l]) + bias)

    def keep_twice(ref, v):
        for i in range(walkers):
            one = v[i * ne:(i + 1) * ne]
            ref[i] = jnp.concatenate([one, one], axis=0).astype(BF16)

    a0 = layer(hid0, 0)
    h1 = hid0 + a0
    a1 = layer(h1, 1)
    a0_ref[...] = a0
    a1_ref[...] = a1
    h1_ref[...] = h1.astype(BF16)
    s0 = 1.0 - a0 * a0
    s1 = 1.0 - a1 * a1
    cr = coeff_rows()
    gl2 = -0.5 * cr
    gl1 = gl2 + mm((s1 * gl2).astype(BF16), wt_ref[...])
    gl1_ref[...] = gl1
    keep_twice(s0_ref, s0)
    keep_twice(s1_ref, s1)
    keep_twice(amp1_ref, -cr * s1)
    keep_twice(b1_ref, 2.0 * cr * a1 * s1)
    keep_twice(b0_ref, -4.0 * a0 * s0 * gl1)
    gw_ref[...] = jnp.zeros_like(gw_ref)

    tangents_u = tangents // SUBS
    pairs = tangents_u // 2
    span = tangents_u * ne
    units = [(w, p) for w in range(walkers) for p in range(SUBS)]

    def split(v):
        return v.reshape(pairs, two, width)

    def flat(v):
        return v.reshape(pairs * two, width)

    def fold(v):
        half = v[:pairs // 2] + v[pairs // 2:]
        total = jnp.sum(half.astype(F32), axis=0)
        return total[:ne] + total[ne:]

    def rows_of(p, v):
        a = jnp.broadcast_to(v[2 * p:2 * p + 1], (lo, width)).astype(BF16)
        b = jnp.broadcast_to(v[2 * p + 1:2 * p + 2], (two - lo - 16, width)).astype(BF16)
        mid = jnp.concatenate([jnp.broadcast_to(v[2 * p:2 * p + 1], (ne - lo, width)),
                               jnp.broadcast_to(v[2 * p + 1:2 * p + 2], (16 - ne + lo, width))], axis=0)
        return jnp.concatenate([a, mid.astype(BF16), b], axis=0)

    def add(u, ref, v):
        w, p = units[u]
        ref[w] = v if p == 0 else ref[w] + v

    def tan0_of(u):
        return tan_ref[u * span:(u + 1) * span, :]

    n = len(units)
    z0, tan1, z1, gb, gz1, back, gz0 = ([None] * n for _ in range(7))

    def start(u):
        z0[u] = split(mm(tan0_of(u), w_ref[0]).astype(BF16))

    def first(u):
        w = units[u][0]
        add(u, sq0_ref, fold(z0[u] * z0[u]))
        tan1[u] = split(tan0_of(u)) + s0_ref[w][None] * z0[u]

    def second(u):
        z1[u] = split(mm(flat(tan1[u]), w_ref[1]).astype(BF16))

    def third(u):
        w = units[u][0]
        add(u, sq1_ref, fold(z1[u] * z1[u]))
        tan2 = tan1[u] + s1_ref[w][None] * z1[u]
        cols = jnp.sum(flat(tan2).astype(F32).reshape(tangents_u, ne, width), axis=1)
        g = jnp.sum(cols * read, axis=1, keepdims=True)
        squares = jnp.broadcast_to(jnp.sum(g * g, axis=0, keepdims=True), (1, width))
        add(u, acc_ref, jnp.concatenate([squares, jnp.sum(g * cols, axis=0, keepdims=True)], axis=0))
        gb[u] = jnp.broadcast_to(g, (tangents_u, width))

    def fourth(u):
        w = units[u][0]
        gains = jnp.stack([rows_of(p, gb[u]) for p in range(pairs)])
        add(u, x1_ref, fold(gains * z1[u]))
        gz1[u] = flat(gains * amp1_ref[w][None] + b1_ref[w][None] * z1[u])

    def fifth(u):
        back[u] = split(mm(gz1[u], wt_ref[...]).astype(BF16))

    def outer1(u):
        gw_ref[1] += outer(flat(tan1[u]), gz1[u])

    def sixth(u):
        w = units[u][0]
        pull = gb[u] * (-coeff(w) * read)
        gt1 = back[u] + jnp.stack([rows_of(p, pull) for p in range(pairs)])
        add(u, x0_ref, fold(gt1 * z0[u]))
        gz0[u] = flat(s0_ref[w][None] * gt1 + b0_ref[w][None] * z0[u])

    def outer0(u):
        gw_ref[0] += outer(tan0_of(u), gz0[u])

    stages = [(start,), (first,), (second,), (third,), (fourth,), (fifth, outer1), (sixth,), (outer0,)]
    for tick in range(n + len(stages) - 1):
        for k in reversed(range(len(stages))):
            if 0 <= tick - k < n:
                for f in stages[k]:
                    f(tick - k)

    share = 1.0 / GROUP
    spin = spin_column()
    cr = coeff_rows()
    gl2 = -0.5 * cr
    a0, a1, gl1 = a0_ref[...], a1_ref[...], gl1_ref[...]
    s0 = 1.0 - a0 * a0
    s1 = 1.0 - a1 * a1
    whole = lambda ref: ref[...].reshape(walkers * ne, width)
    sq0, sq1 = whole(sq0_ref), whole(sq1_ref)
    lap0 = lap_ref[...]
    lb0 = lap0.astype(BF16)
    lz0 = mm(lb0, w_ref[0])
    lap1 = share * (lap0 + s0 * lz0) - 2.0 * a0 * s0 * sq0
    lb1 = lap1.astype(BF16)
    lz1 = mm(lb1, w_ref[1])
    lap2 = lap1 + s1 * lz1 - 2.0 * a1 * s1 * sq1
    glz1 = (s1 * gl2).astype(BF16)
    glz0 = (s0 * gl1).astype(BF16)
    gs1 = gl2 * lz1 - cr * whole(x1_ref)
    gz1 = (-2.0 * a1 * gs1 + (6.0 * a1 * a1 - 2.0) * gl2 * sq1) * s1
    gz1b = gz1.astype(BF16)
    gw_ref[1] += outer(h1_ref[...], gz1b) + outer(lb1, glz1)
    gh1 = mm(gz1b, wt_ref[...])
    gs0 = gl1 * (share * lz0) + whole(x0_ref)
    gz0 = (-2.0 * a0 * gs0 + (6.0 * a0 * a0 - 2.0) * gl1 * sq0 + gh1) * s0
    gw_ref[0] += outer(hid_ref[...].astype(BF16), gz0.astype(BF16)) + share * outer(lb0, glz0)
    lapsum = jnp.sum(lap2.reshape(walkers, ne, width), axis=1)
    small = []
    for gz in (gz0, gz1):
        for s in range(2):
            small.append(jnp.sum(jnp.where(spin == s, gz, 0.0), axis=0, keepdims=True))
    gread = jnp.zeros((1, width), F32)
    energy = []
    for i in range(walkers):
        gread -= coeff(i) * (0.5 * lapsum[i:i + 1] + acc_ref[i, 1:2, :])
        energy.append(-0.5 * (jnp.sum(lapsum[i:i + 1] * read, axis=1, keepdims=True) + acc_ref[i, 0:1, 0:1]))
    lane = lax.broadcasted_iota(jnp.int32, (1, LANES), 1)
    here = HALF + walkers * x_index()
    slots = jnp.zeros((1, LANES), F32)
    for i in range(walkers):
        slots = jnp.where(lane == here + i, energy[i], slots)
    extras = [small_part(small + [gread], q, slots, lane) for q in range(NX)]
    block = width // GROUP
    own = core_index()
    for ref, core, sign in ((mine_ref, own, -1.0), (theirs_ref, 1 - own, 1.0)):
        for n, (y, q) in enumerate(YX_ORDER):
            at = pl.multiple_of((y * NC + core) * block, block)
            l, sub = divmod(q, 2)
            rows_q = sign * gw_ref[l, pl.ds(at + 8 * sub, 8), :]
            base = PIECE * n
            ref[base:base + 8, :] = rows_q[:, :LANES]
            ref[base + 8:base + 16, :] = rows_q[:, LANES:]
            ref[base + 16:base + PIECE, :] = sign * extras[q]


def small_part(small, q, slots, lane):
    half, sub = divmod(q, 2)

    def low(r):
        v = small[r][:, half * LANES:(half + 1) * LANES]
        return pltpu.roll(v, HALF, 1) if sub else v

    def high(r):
        v = small[r][:, half * LANES:(half + 1) * LANES]
        return v if sub else pltpu.roll(v, HALF, 1)

    first = lane < HALF
    return jnp.concatenate([jnp.where(first, low(0), high(1)), jnp.where(first, low(2), high(3)),
                            jnp.where(first, low(4), slots)], axis=0)


def x_index():
    return lax.axis_index("x")


def core_index():
    return lax.axis_index("core")


def local_part(hidden0, tangent0, laplace0, spins, weights, spin_bias, readout, cot):
    walkers, tangents, ne, width = tangent0.shape
    rows = walkers * ne
    half = (NY * NX * PIECE, LANES)
    body = functools.partial(local_kernel, walkers=walkers, tangents=tangents, ne=ne, width=width,
                             walkers_all=walkers * NX * NZ)
    full = lambda *shape: pl.BlockSpec(shape, lambda w: (0,) * len(shape))
    wide = pltpu.VMEM((rows, width), F32)
    twice = pltpu.VMEM((walkers, 2 * ne, width), BF16)
    sums = pltpu.VMEM((walkers, ne, width), F32)
    return pl.pallas_call(
        body,
        grid=(1,),
        out_shape=[jax.ShapeDtypeStruct(half, F32)] * 2,
        in_specs=[
            pl.BlockSpec(memory_space=pltpu.SMEM),
            full(walkers * tangents * ne, width),
            full(rows, width),
            full(rows, width),
            full(walkers, ne),
            full(2, width, width),
            full(2, 2, width),
            full(1, width),
        ],
        out_specs=[full(*half)] * 2,
        scratch_shapes=[pltpu.VMEM((width, width), BF16)] + [wide] * 3 + [pltpu.VMEM((rows, width), BF16)]
        + [twice] * 5 + [sums] * 4 + [pltpu.VMEM((2, width, width), F32), pltpu.VMEM((walkers, 2, width), F32)],
        compiler_params=pltpu.CompilerParams(vmem_limit_bytes=60 * 1024 * 1024),
        name="local_part",
    )(cot, tangent0.reshape(-1, width), hidden0.reshape(rows, width), laplace0.reshape(rows, width),
      spins, weights, spin_bias, readout.reshape(1, width))


def last_sum_kernel(parts_ref, own_ref, energy_ref, weights_ref, bias_ref, read_ref):
    walkers = energy_ref.shape[0]
    totals = []
    for q in range(NX):
        pieces = [parts_ref[PIECE * n:PIECE * (n + 1), :] for n, (x, _) in enumerate(XZ_ORDER) if x == q]
        total = sum(pieces[1:], pieces[0])
        l, sub = divmod(q, 2)
        weights_ref[l, 8 * sub:8 * sub + 8, :LANES] = total[:8]
        weights_ref[l, 8 * sub:8 * sub + 8, LANES:] = total[8:16]
        totals.append(total[16:])
    lane = lax.broadcasted_iota(jnp.int32, (1, LANES), 1)
    first = lane < HALF

    def small_row(r):
        at = slice(r // 2, r // 2 + 1)
        halves = []
        for half in range(2):
            a, b = totals[2 * half][at], totals[2 * half + 1][at]
            if r % 2 == 0:
                b = pltpu.roll(b, HALF, 1)
            else:
                a = pltpu.roll(a, HALF, 1)
            halves.append(jnp.where(first, a, b))
        return jnp.concatenate(halves, axis=1)

    for l in range(2):
        bias_ref[l] = jnp.concatenate([small_row(2 * l), small_row(2 * l + 1)], axis=0)
    read_ref[...] = small_row(4)[0]
    slots = own_ref[PIECE - 1:PIECE, :]
    here = HALF + walkers * x_index()
    spread = jnp.zeros((1, LANES), F32)
    for i in range(walkers):
        one = jnp.sum(jnp.where(lane == here + i, slots, 0.0), axis=1, keepdims=True)
        spread = jnp.where(lane == i, one, spread)
    energy_ref[...] = spread[0, :walkers]


def last_sum(parts, own, walkers, width):
    shapes = ((walkers,), (2, width // GROUP, width), (2, 2, width), (width,))
    return pl.pallas_call(
        last_sum_kernel,
        out_shape=[jax.ShapeDtypeStruct(s, F32) for s in shapes],
        compiler_params=pltpu.CompilerParams(vmem_limit_bytes=4 * 1024 * 1024),
        name="last_sum",
    )(parts.reshape(-1, LANES), own.reshape(PIECE, LANES))


def exchange(pieces, axes, order):
    return lax.all_to_all(pieces, axes, 0, 0, axis_index_groups=[order])


def per_device(hidden0, tangent0, laplace0, spins, weights, spin_bias, readout, energy_cotangent):
    walkers = hidden0.shape[0]
    width = weights.shape[1]
    minus, theirs = local_part(hidden0, tangent0, laplace0, spins, weights, spin_bias, readout, energy_cotangent)
    got = lax.ppermute(theirs, "core", [(0, 1), (1, 0)])
    part = (lax.optimization_barrier(-minus) + got).reshape(NY * NX, PIECE, 1, LANES)
    own = jnp.sum(exchange(part, ("y", "x"), [y * NX + x for y, x in YX_ORDER]), axis=0)
    part = jnp.broadcast_to(own[None], (NX * NZ,) + own.shape)
    return last_sum(exchange(part, ("x", "z"), [x * NZ + z for x, z in XZ_ORDER]), own, walkers, width)


def solution(mesh):
    split = Mesh(mesh.devices.reshape(NX, NZ, NY, NC), ("x", "z", "y", "core"))
    walker, tangent = ("x", "z"), ("y", "core")
    in_specs = (
        P(walker, None, None),
        P(walker, tangent, None, None),
        P(walker, None, None),
        P(walker, None),
        P(),
        P(),
        P(),
        P(walker),
    )
    out_specs = (P(walker), P(None, tangent, None), P(), P())
    return jax.shard_map(
        per_device, mesh=split, in_specs=in_specs, out_specs=out_specs, check_vma=False
    )
```
